32 devices in a mesh: ctx: 16 (over z, x, core), head: 2 (over y).
Axes of the slice: x: 2, y: 2, z: 4, core: 2. Of those that a mesh axis runs over, the one named last changes fastest.
Arguments:
- queries: bfloat16 [4096, 2048], P(('ctx', 'head')), may hold values from -8.5 to 8.5
- keys: bfloat16 [4096, 1024], P(('ctx', 'head')), may hold values from -8.5 to 8.5
- values: bfloat16 [4096, 1024], P(('ctx', 'head')), may hold values from -5 to 5
- grad_attn: bfloat16 [4096, 2048], P(('ctx', 'head')), may hold values from -5 to 5
- parent_gap: int32 [16], replicated, may hold values from 0 to 2, as said below
Outputs:
- attended: bfloat16 [4096, 2048], P(('ctx', 'head'))
- grad_query: bfloat16 [4096, 2048], P(('ctx', 'head'))
- grad_key: bfloat16 [4096, 1024], P(('ctx', 'head'))
- grad_value: bfloat16 [4096, 1024], P(('ctx', 'head'))
The draws below stay inside these ranges and needn't reach their ends.
Inputs may be any that keep to these rules, and one draw needn't show every extreme that they name: Shards are in depth-first order of a tree rooted at shard 0: the parent of shard s > 0 is shard s - parent_gap[s], and parent_gap[0] = 0. The ancestor 4 levels above a shard, where it exists, lies at most 8 shards before it.
All inputs are finite; a program needn't handle non-finite values.
Results may differ from the reference program's by a relative error of at most 0.011.
Values may be sent and summed in bfloat16 or wider, within the bound.
A program may use at most 128 MiB of HBM per device.

```python
import math
import jax
import jax.numpy as jnp
from jax import lax

HD = 256
KVH = 4
GROUP = 2
FORK = 2
TOK_DEV = 256
QH = 8
LEVELS = 4
SHARDS = 16
TOKENS = 4096


def query_key_pair(key):
    shape_query = (TOKENS, KVH, GROUP, HD)
    shape_key = (TOKENS, KVH, HD)
    query = jax.random.truncated_normal(jax.random.fold_in(key, 21), -4.0, 4.0, shape_query, jnp.float32)
    key_base = jax.random.truncated_normal(jax.random.fold_in(key, 22), -4.0, 4.0, shape_key, jnp.float32)
    return (query.reshape(TOKENS, KVH * GROUP * HD), key_base.reshape(TOKENS, KVH * HD))


def draw_queries(key, part):
    return query_key_pair(key)[0].astype(jnp.bfloat16)


def draw_keys(key, part):
    return query_key_pair(key)[1].astype(jnp.bfloat16)


def draw_parent_gap(key, part):
    leaves = jax.random.randint(jax.random.fold_in(key, 31), (SHARDS,), 0, FORK)
    leeway = (SHARDS - 1) // FORK - LEVELS + 1
    forced_start = jax.random.randint(jax.random.fold_in(key, 32), (), 0, leeway)
    ordinal = jnp.arange(SHARDS, dtype=jnp.int32)
    forced = jnp.logical_and(ordinal >= forced_start, ordinal < forced_start + LEVELS)
    leaves = jnp.where(forced, FORK - 1, leaves)
    length = leaves + 1
    starts = jnp.cumsum(length) - length
    member = jnp.sum((starts[None, :] <= ordinal[:, None]).astype(jnp.int32), 1) - 1
    within = ordinal - jnp.take(starts, member)
    before = jnp.take(length, jnp.maximum(member - 1, 0))
    gaps = jnp.where(within > 0, within, jnp.where(member > 0, before, 0))
    return gaps.astype(jnp.int32)


def block_scale(key, dims, cuts, least, top_value):
    factor_of = 1.0
    for dim, blocks in cuts:
        heights = jax.random.uniform(jax.random.fold_in(jax.random.fold_in(key, 6), dim), (blocks,), jnp.float32, least / len(cuts), top_value / len(cuts))
        factor_of = factor_of * jnp.repeat(jnp.exp(heights), dims[dim] // blocks).reshape((-1,) + (1,) * (len(dims) - 1 - dim))
    return factor_of


def normal_values(own_key, shape, scale, limit, split=(), held_as=jnp.bfloat16):
    gain = block_scale(own_key, shape, split, -0.22, 0.18) if split else 1.0
    entries = jax.random.normal(own_key, shape, jnp.float32) * scale * gain
    return jnp.minimum(jnp.maximum(entries, -limit), limit).astype(held_as)


def setup_inputs(seed: int = 0) -> dict:
    splits = jax.random.split(jax.random.key(seed), 6)
    queries = draw_queries(jax.random.fold_in(splits[5], 71), 0)
    keys = draw_keys(jax.random.fold_in(splits[5], 71), 0)
    values = normal_values(splits[2], (TOKENS, KVH * HD), 1.0, 5.0, ((0, 32),))
    grad_attn = normal_values(splits[3], (TOKENS, QH * HD), 1.0, 5.0, ((0, 32),))
    parent_gap = draw_parent_gap(jax.random.fold_in(splits[5], 71), 0)
    return dict(queries=queries, keys=keys, values=values, grad_attn=grad_attn, parent_gap=parent_gap)


BASE = 10000.0


def tree_tables(parent_gap):
    shard_count = parent_gap.shape[0]
    ordinal = jnp.arange(shard_count, dtype=jnp.int32)
    parent = jnp.where(parent_gap > 0, ordinal - parent_gap, shard_count).astype(jnp.int32)
    pointer = jnp.concatenate([parent, jnp.full((1,), shard_count, jnp.int32)])
    depths = jnp.concatenate([(parent_gap > 0).astype(jnp.int32), jnp.zeros((1,), jnp.int32)])
    jumped = pointer
    for rounds in range(shard_count.bit_length()):
        depths = depths + jnp.take(depths, jumped)
        jumped = jnp.take(jumped, jumped)
    return pointer, depths


def rotate(inputs, position, direction):
    half_dim = inputs.shape[-1] // 2
    frequency = jnp.exp(jnp.arange(half_dim, dtype=jnp.float32) * (-2.0 * math.log(BASE) / inputs.shape[-1]))
    angles = position.astype(jnp.float32)[:, None] * frequency[None, :]
    cosine = jnp.cos(angles)[:, None, :]
    sine_part = direction * jnp.sin(angles)[:, None, :]
    first_half = inputs[..., :half_dim]
    second = inputs[..., half_dim:]
    return jnp.concatenate([first_half * cosine - second * sine_part, second * cosine + first_half * sine_part], -1)


def visible_mask(length, levels, present):
    within = jnp.arange(length, dtype=jnp.int32)
    later_key = within[None, :] > within[:, None]
    blocks_list = [jnp.logical_not(later_key)]
    for height in range(1, levels + 1):
        blocks_list.append(jnp.logical_and(present[height - 1], jnp.logical_or(height < levels, later_key)))
    return jnp.stack(blocks_list, 1).reshape(length, (levels + 1) * length)


def attend_exact(query, key_all, value_all, grad_out, visible):
    scaling = query.shape[-1] ** -0.5
    query32 = query.astype(jnp.float32)
    key32 = key_all.astype(jnp.float32)
    value32 = value_all.astype(jnp.float32)
    grad32 = grad_out.astype(jnp.float32)
    scores = jnp.einsum("tkgd,ukd->kgtu", query32, key32) * scaling
    scores = jnp.where(visible, scores, -1e30)
    highest = jnp.max(scores, -1, keepdims=True)
    raw_weights = jnp.where(visible, jnp.exp(scores - highest), 0.0)
    probabilities = raw_weights / jnp.sum(raw_weights, -1, keepdims=True)
    probs_low = probabilities.astype(jnp.bfloat16)
    attended = jnp.einsum("kgtu,ukd->tkgd", probs_low.astype(jnp.float32), value32).astype(jnp.bfloat16)
    grad_prob = jnp.einsum("tkgd,ukd->kgtu", grad32, value32)
    row_delta = jnp.sum(probabilities * grad_prob, -1, keepdims=True)
    grad_score = (probabilities * (grad_prob - row_delta) * scaling).astype(jnp.bfloat16)
    score32 = grad_score.astype(jnp.float32)
    grad_qrot = jnp.einsum("kgtu,ukd->tkgd", score32, key32)
    part_key = jnp.einsum("kgtu,tkgd->ukd", score32, query32)
    part_value = jnp.einsum("kgtu,tkgd->ukd", probs_low.astype(jnp.float32), grad32)
    return attended, grad_qrot, part_key, part_value


def reference(queries, keys, values, grad_attn, parent_gap):
    pointer, depths = tree_tables(parent_gap)
    ordinal = jnp.arange(SHARDS, dtype=jnp.int32)
    elders = []
    current = pointer[:SHARDS]
    for height in range(LEVELS):
        elders.append(current)
        current = jnp.take(pointer, current)
    elders = jnp.stack(elders, 1)
    present = elders < SHARDS
    table = jnp.concatenate([ordinal[:, None], jnp.where(present, elders, 0)], 1).astype(jnp.int32)
    within = jnp.arange(TOK_DEV, dtype=jnp.int32)
    position = (depths[:SHARDS, None] * TOK_DEV + within[None, :]).reshape(TOKENS)
    query_rot = rotate(queries.astype(jnp.float32).reshape(TOKENS, QH, HD), position, 1.0).astype(jnp.bfloat16)
    query_rot = query_rot.reshape(SHARDS, TOK_DEV, KVH, GROUP, HD)
    key_rot = rotate(keys.astype(jnp.float32).reshape(TOKENS, KVH, HD), position, 1.0).astype(jnp.bfloat16)
    key_rot = key_rot.reshape(SHARDS, TOK_DEV, KVH, HD)
    value_shards = values.reshape(SHARDS, TOK_DEV, KVH, HD)
    grad_shards = grad_attn.reshape(SHARDS, TOK_DEV, KVH, GROUP, HD)
    shard_positions = position.reshape(SHARDS, TOK_DEV)

    def shard_step(carry, shard_id):
        total_key, total_value = carry
        chosen = table[shard_id]
        key_all = jnp.take(key_rot, chosen, axis=0).reshape((LEVELS + 1) * TOK_DEV, KVH, HD)
        value_all = jnp.take(value_shards, chosen, axis=0).reshape((LEVELS + 1) * TOK_DEV, KVH, HD)
        visible = visible_mask(TOK_DEV, LEVELS, present[shard_id])
        attended, grad_qrot, part_key, part_value = attend_exact(query_rot[shard_id], key_all, value_all, grad_shards[shard_id], visible)
        total_key = total_key.at[chosen].add(part_key.reshape(LEVELS + 1, TOK_DEV, KVH, HD))
        total_value = total_value.at[chosen].add(part_value.reshape(LEVELS + 1, TOK_DEV, KVH, HD))
        grad_query = rotate(grad_qrot.reshape(TOK_DEV, QH, HD), shard_positions[shard_id], -1.0).astype(jnp.bfloat16)
        return (total_key, total_value), (attended.reshape(TOK_DEV, QH * HD), grad_query.reshape(TOK_DEV, QH * HD))

    zeros = jnp.zeros((SHARDS, TOK_DEV, KVH, HD), jnp.float32)
    (total_key, total_value), (attended, grad_query) = lax.scan(shard_step, (zeros, zeros), ordinal)
    grad_key = rotate(total_key.reshape(TOKENS, KVH, HD), position, -1.0).astype(jnp.bfloat16).reshape(TOKENS, KVH * HD)
    grad_value = total_value.astype(jnp.bfloat16).reshape(TOKENS, KVH * HD)
    return attended.reshape(TOKENS, QH * HD), grad_query.reshape(TOKENS, QH * HD), grad_key, grad_value
```

```python
import functools
import math

import jax
import jax.numpy as jnp
from jax import lax
from jax.experimental import pallas as pl
from jax.experimental.pallas import tpu as pltpu
from jax.sharding import PartitionSpec as P

HD = 256
GROUP = 2
WINDOW = 1024
FORK = 2
BASE = 10000.0
SLOTS = 9
VMEM_LIMIT = 48 * 2**20
MESH = pl.DeviceIdType.MESH


def tree_tables(parent_gap, own_shard, levels):
    count = parent_gap.shape[0]
    ordinal = jnp.arange(count, dtype=jnp.int32)
    deeper = (parent_gap == 1).astype(jnp.int32)
    depths = jnp.sum(jnp.where(ordinal[None, :] <= ordinal[:, None], deeper[None, :], 0), 1)
    depth = jnp.sum(jnp.where(ordinal <= own_shard, deeper, 0))
    height = jnp.arange(levels + 1, dtype=jnp.int32)
    match = jnp.logical_and(
        depths[None, :] == depth - height[:, None], ordinal[None, :] <= own_shard
    )
    elder = jnp.max(jnp.where(match, ordinal[None, :], -1), 1)
    present = elder >= 0
    slot = jnp.where(present, own_shard - elder, 0)
    return depth, slot.astype(jnp.int32), present.astype(jnp.int32)


def angles(depth, tokens):
    half = HD // 2
    position = depth * tokens + jnp.arange(tokens, dtype=jnp.int32)
    frequency = jnp.exp(jnp.arange(half, dtype=jnp.float32) * (-2.0 * math.log(BASE) / HD))
    angle = position.astype(jnp.float32)[:, None] * frequency[None, :]
    return jnp.cos(angle), jnp.sin(angle)


def turn(block, cosine, sine):
    half = HD // 2
    first, second = block[:, :half], block[:, half:]
    return jnp.concatenate([first * cosine - second * sine, second * cosine + first * sine], -1)


def greet(shards, heads):
    me, head = lax.axis_index("ctx"), lax.axis_index("head")
    core, row = lax.rem(me, 2), lax.rem(me // 2, 2)
    barrier = pltpu.get_barrier_semaphore()
    up, down = me + 4 < shards, me >= 4
    for step in range(1, heads):
        pl.semaphore_signal(
            barrier, inc=1, device_id={"head": lax.rem(head + step, heads)}, device_id_type=MESH
        )
    for other in (me + 1 - 2 * core, me + 2 - 4 * row):
        pl.semaphore_signal(barrier, inc=1, device_id={"ctx": other}, device_id_type=MESH)

    @pl.when(up)
    def _():
        pl.semaphore_signal(barrier, inc=1, device_id={"ctx": me + 4}, device_id_type=MESH)

    @pl.when(down)
    def _():
        pl.semaphore_signal(barrier, inc=1, device_id={"ctx": me - 4}, device_id_type=MESH)

    pl.semaphore_wait(barrier, heads + 1 + up.astype(jnp.int32) + down.astype(jnp.int32))
    return me, head, core, row


def both(*terms):
    return functools.reduce(jnp.logical_and, terms)


def remote(src, dst, send_sem, recv_sem, device):
    return pltpu.make_async_remote_copy(
        src_ref=src,
        dst_ref=dst,
        send_sem=send_sem,
        recv_sem=recv_sem,
        device_id=device,
        device_id_type=MESH,
    )


def gather_kernel(
    shards, heads, q, k, v, g, cosine, sine, qh, gh, kb, vb,
    qr, kr, y_send, y_recv, y_local, c_send, c_recv,
):
    me, head, core, row = greet(shards, heads)
    rows = q.shape[0]
    mine = pl.ds(pl.multiple_of(head * rows, rows), rows)
    cos, sin = cosine[mine, :], sine[mine, :]

    def rotate(src, dst):
        for i in range(src.shape[1] // HD):
            at = slice(i * HD, (i + 1) * HD)
            dst[:, at] = turn(src[:, at].astype(jnp.float32), cos, sin).astype(jnp.bfloat16)

    exchanged = {}

    def exchange(index, src, dst):
        width = src.shape[1] // heads
        copies = []
        for step in range(1, heads):
            peer = lax.rem(head + step, heads)
            columns = pl.ds(pl.multiple_of(peer * width, width), width)
            copies.append(
                remote(
                    src.at[:, columns], dst.at[mine, :],
                    y_send.at[index, step - 1], y_recv.at[index, step - 1], {"head": peer},
                )
            )
        columns = pl.ds(pl.multiple_of(head * width, width), width)
        local = pltpu.make_async_copy(src.at[:, columns], dst.at[mine, :], y_local.at[index])
        for copy in copies:
            copy.start()
        local.start()
        exchanged[index] = (copies, local)

    def arrived(index):
        copies, local = exchanged[index]
        local.wait()
        for copy in copies:
            copy.wait_recv()

    buffers = (kb, vb)
    sends = []

    def send(kv, src, dst, target, *conditions):
        copy = remote(
            buffers[kv].at[src], buffers[kv].at[dst],
            c_send.at[len(sends)], c_recv.at[kv, dst], {"ctx": target},
        )
        condition = both(me >= src, *conditions)
        pl.when(condition)(copy.start)
        sends.append((condition, copy))

    def received(kv, slot):
        copy = remote(
            buffers[kv].at[slot], buffers[kv].at[slot],
            c_send.at[0], c_recv.at[kv, slot], {"ctx": me + 1 - 2 * core},
        )
        pl.when(me >= slot)(copy.wait_recv)

    rotate(k, kr)
    exchange(0, kr, kb.at[0])
    exchange(1, v, vb.at[0])
    rotate(q, qr)
    up = me + 4 < shards
    for kv in (0, 1):
        arrived(kv)
        send(kv, 0, 4, me + 4, up)
        send(kv, 0, 2, me + 2, row == 0)
        send(kv, 0, 1, me + 1, core == 0)
    exchange(2, qr, qh)
    exchange(3, g, gh)
    for kv in (0, 1):
        received(kv, 4)
        send(kv, 4, 8, me + 4, up)
        send(kv, 4, 6, me + 2, row == 0)
        send(kv, 4, 2, me - 2, row == 1)
        send(kv, 4, 5, me + 1, core == 0)
        send(kv, 4, 3, me - 1, core == 1)
    for kv in (0, 1):
        received(kv, 2)
        send(kv, 2, 3, me + 1, core == 0)
        send(kv, 2, 1, me - 1, core == 1)
    for kv in (0, 1):
        received(kv, 8)
        send(kv, 8, 6, me - 2, row == 1)
        send(kv, 8, 7, me - 1, core == 1)
    for kv in (0, 1):
        received(kv, 6)
        send(kv, 6, 7, me + 1, core == 0)
        send(kv, 6, 5, me - 1, core == 1)
    arrived(2)
    arrived(3)
    for slot in (1, 3, 5, 7):
        for kv in (0, 1):
            received(kv, slot)
    for condition, copy in sends:
        pl.when(condition)(copy.wait_send)
    for copies, _ in exchanged.values():
        for copy in copies:
            copy.wait_send()


def gather(shards, heads, q, k, v, g, cosine, sine):
    rows = q.shape[0]
    tokens = rows * heads
    wide, narrow = q.shape[1] // heads, k.shape[1] // heads
    vmem = pl.BlockSpec(memory_space=pltpu.VMEM)
    hbm = pl.BlockSpec(memory_space=pl.ANY)
    low = jnp.bfloat16
    return pl.pallas_call(
        functools.partial(gather_kernel, shards, heads),
        out_shape=[
            jax.ShapeDtypeStruct((tokens, wide), low),
            jax.ShapeDtypeStruct((tokens, wide), low),
            jax.ShapeDtypeStruct((SLOTS, tokens, narrow), low),
            jax.ShapeDtypeStruct((SLOTS, tokens, narrow), low),
        ],
        in_specs=[vmem] * 6,
        out_specs=[hbm] * 4,
        scratch_shapes=[
            pltpu.VMEM(q.shape, low),
            pltpu.VMEM(k.shape, low),
            pltpu.SemaphoreType.DMA((4, heads - 1)),
            pltpu.SemaphoreType.DMA((4, heads - 1)),
            pltpu.SemaphoreType.DMA((4,)),
            pltpu.SemaphoreType.DMA((28,)),
            pltpu.SemaphoreType.DMA((2, SLOTS)),
        ],
        compiler_params=pltpu.CompilerParams(
            collective_id=0, has_side_effects=True, vmem_limit_bytes=VMEM_LIMIT
        ),
        name="gather",
    )(q, k, v, g, cosine, sine)


def attend_kernel(levels, table, *refs):
    q, g = refs[:2]
    keys, values = refs[2 : 3 + levels], refs[3 + levels : 4 + 2 * levels]
    cosine, sine, out, grad_q, part_k, part_v = refs[4 + 2 * levels :]
    tokens = q.shape[0]
    scaling = HD**-0.5
    f32, low = jnp.float32, jnp.bfloat16
    query = jnp.concatenate([q[:, i * HD : (i + 1) * HD] for i in range(GROUP)], 0)
    grad = jnp.concatenate([g[:, i * HD : (i + 1) * HD] for i in range(GROUP)], 0)
    across = (((1,), (1,)), ((), ()))
    down = (((0,), (0,)), ((), ()))
    key_at = lax.broadcasted_iota(jnp.int32, (tokens, tokens), 1)
    query_at = lax.broadcasted_iota(jnp.int32, (tokens, tokens), 0)
    later = jnp.concatenate([(key_at - query_at).astype(f32)] * GROUP, 0) > 0
    scores = []
    for j in range(levels + 1):
        s = lax.dot_general(query, keys[j][0], across, preferred_element_type=f32) * scaling
        if j == 0:
            s = jnp.where(later, -1e30, s)
        else:
            if j == levels:
                s = jnp.where(later, s, -1e30)
            s = jnp.where(table[levels + 1 + j] > 0, s, -1e30)
        scores.append(s)
    highest = functools.reduce(jnp.maximum, [jnp.max(s, -1, keepdims=True) for s in scores])
    raw = [jnp.exp(s - highest) for s in scores]
    total = sum(jnp.sum(r, -1, keepdims=True) for r in raw)
    inverse = 1.0 / total
    probs = [r * inverse for r in raw]
    probs_low = [p.astype(low) for p in probs]
    attended = sum(
        lax.dot(p, values[j][0], preferred_element_type=f32) for j, p in enumerate(probs_low)
    )
    grad_probs = [
        lax.dot_general(grad, values[j][0], across, preferred_element_type=f32)
        for j in range(levels + 1)
    ]
    delta = sum(jnp.sum(p * d, -1, keepdims=True) for p, d in zip(probs, grad_probs))
    grad_scores = [
        (p * (d - delta) * scaling).astype(low) for p, d in zip(probs, grad_probs)
    ]
    turned = sum(
        lax.dot(d, keys[j][0], preferred_element_type=f32) for j, d in enumerate(grad_scores)
    )
    cos, sin = cosine[...], -sine[...]
    for i in range(GROUP):
        rows, at = slice(i * tokens, (i + 1) * tokens), slice(i * HD, (i + 1) * HD)
        out[:, at] = attended[rows].astype(low)
        grad_q[:, at] = turn(turned[rows], cos, sin).astype(low)
    part_k[...] = jnp.zeros_like(part_k)
    part_v[...] = jnp.zeros_like(part_v)
    for j in range(levels + 1):

        def put(j=j):
            slot = table[j]
            part_k[slot] = lax.dot_general(
                grad_scores[j], query, down, preferred_element_type=f32
            ).astype(low)
            part_v[slot] = lax.dot_general(
                probs_low[j], grad, down, preferred_element_type=f32
            ).astype(low)

        pl.when(table[levels + 1 + j] > 0)(put)


def attend(levels, table, qh, gh, kb, vb, cosine, sine):
    tokens = qh.shape[0]
    kv_local = kb.shape[2] // HD
    low = jnp.bfloat16

    def chosen(j):
        return pl.BlockSpec((1, tokens, HD), lambda h, t: (t[j], 0, h))

    wide = pl.BlockSpec((tokens, GROUP * HD), lambda h, t: (0, h))
    table_spec = pl.BlockSpec((tokens, HD // 2), lambda h, t: (0, 0))
    part = pl.BlockSpec((SLOTS, tokens, HD), lambda h, t: (0, 0, h))
    count = levels + 1
    return pl.pallas_call(
        functools.partial(attend_kernel, levels),
        out_shape=[
            jax.ShapeDtypeStruct(qh.shape, low),
            jax.ShapeDtypeStruct(qh.shape, low),
            jax.ShapeDtypeStruct(kb.shape, low),
            jax.ShapeDtypeStruct(vb.shape, low),
        ],
        grid_spec=pltpu.PrefetchScalarGridSpec(
            num_scalar_prefetch=1,
            grid=(kv_local,),
            in_specs=[wide, wide]
            + [chosen(j) for j in range(count)] * 2
            + [table_spec, table_spec],
            out_specs=[wide, wide, part, part],
        ),
        compiler_params=pltpu.CompilerParams(vmem_limit_bytes=VMEM_LIMIT),
        name="attend",
    )(table, qh, gh, *[kb] * count, *[vb] * count, cosine, sine)


def return_kernel(
    shards, heads, out, grad_q, part_k, part_v, cosine, sine, out_o, out_q, out_k, out_v,
    acc, from_core, from_row, from_up, done, y_send, y_recv, y_local, c_send, c_recv,
):
    me, head, core, row = greet(shards, heads)
    rows = out_o.shape[0]
    f32, low = jnp.float32, jnp.bfloat16
    exchanged = []

    def exchange(src, dst):
        index = len(exchanged)
        width = src.shape[1]
        columns = pl.ds(pl.multiple_of(head * width, width), width)
        copies = []
        for step in range(1, heads):
            peer = lax.rem(head + step, heads)
            theirs = pl.ds(pl.multiple_of(peer * rows, rows), rows)
            copies.append(
                remote(
                    src.at[theirs, :], dst.at[:, columns],
                    y_send.at[index, step - 1], y_recv.at[index, step - 1], {"head": peer},
                )
            )
        mine = pl.ds(pl.multiple_of(head * rows, rows), rows)
        local = pltpu.make_async_copy(src.at[mine, :], dst.at[:, columns], y_local.at[index])
        for copy in copies:
            copy.start()
        local.start()
        exchanged.append((copies, local))

    parts = (part_k, part_v)
    core_copies, row_copies, up_copies = {}, {}, {}
    for i in (3, 2, 1, 0):
        for kv in (0, 1):
            core_copies[kv, i] = remote(
                parts[kv].at[2 * i + 1], from_core.at[kv, i],
                c_send.at[kv, i], c_recv.at[kv, i], {"ctx": me + 1 - 2 * core},
            )
            core_copies[kv, i].start()

    def to_row(kv, i, slot):
        row_copies[kv, i] = remote(
            acc.at[kv, slot // 2], from_row.at[kv, i],
            c_send.at[kv, 4 + i], c_recv.at[kv, 4 + i], {"ctx": me + 2 - 4 * row},
        )
        row_copies[kv, i].start()

    has_down, has_up = me >= 4, me + 4 < shards

    def to_down(kv, i, slot):
        up_copies[kv, i] = remote(
            acc.at[kv, slot // 2], from_up.at[kv, i],
            c_send.at[kv, 6 + i], c_recv.at[kv, 6 + i], {"ctx": me - 4},
        )
        pl.when(has_down)(up_copies[kv, i].start)

    def add(kv, slot, piece):
        at = slot // 2
        acc[kv, at] = (acc[kv, at].astype(f32) + piece.astype(f32)).astype(low)

    def start(kv, slot, piece):
        acc[kv, slot // 2] = (parts[kv][slot].astype(f32) + piece.astype(f32)).astype(low)

    for kv in (0, 1):
        core_copies[kv, 3].wait_recv()
        core_copies[kv, 2].wait_recv()
        start(kv, 6, from_core[kv, 3 - core])
        to_row(kv, 1, 6)
    for kv in (0, 1):

        @pl.when(core == 1)
        def _(kv=kv):
            start(kv, 8, from_core[kv, 3])

        @pl.when(core == 0)
        def _(kv=kv):
            acc[kv, 4] = parts[kv][8]

        core_copies[kv, 1].wait_recv()
        core_copies[kv, 0].wait_recv()
        start(kv, 2, from_core[kv, 1 - core])
        to_row(kv, 0, 2)
    exchange(out, out_o)
    exchange(grad_q, out_q)
    for kv in (0, 1):
        start(kv, 4, from_core[kv, 2 - core])

        @pl.when(core == 0)
        def _(kv=kv):
            start(kv, 0, from_core[kv, 0])

        @pl.when(core == 1)
        def _(kv=kv):
            acc[kv, 0] = parts[kv][0]

    for kv in (0, 1):
        row_copies[kv, 1].wait_recv()

        @pl.when(row == 1)
        def _(kv=kv):
            add(kv, 8, from_row[kv, 1])

        @pl.when(row == 0)
        def _(kv=kv):
            add(kv, 4, from_row[kv, 1])

        to_down(kv, 1, 8)
    for kv in (0, 1):
        row_copies[kv, 0].wait_recv()

        @pl.when(row == 1)
        def _(kv=kv):
            add(kv, 4, from_row[kv, 0])

        @pl.when(row == 0)
        def _(kv=kv):
            add(kv, 0, from_row[kv, 0])

        @pl.when(has_up)
        def _(kv=kv):
            up_copies[kv, 1].wait_recv()
            add(kv, 4, from_up[kv, 1])

        to_down(kv, 0, 4)
    for kv in (0, 1):

        @pl.when(has_up)
        def _(kv=kv):
            up_copies[kv, 0].wait_recv()
            add(kv, 0, from_up[kv, 0])

        if kv == 0:
            cos, sin = cosine[...], -sine[...]
            for i in range(acc.shape[3] // HD):
                at = slice(i * HD, (i + 1) * HD)
                done[kv, :, at] = turn(acc[kv, 0, :, at].astype(f32), cos, sin).astype(low)
        else:
            done[kv] = acc[kv, 0]
        exchange(done.at[kv], (out_k, out_v)[kv])
    for copies, local in exchanged:
        for copy in copies:
            copy.wait()
        local.wait()
    for copies in (core_copies, row_copies):
        for copy in copies.values():
            copy.wait_send()
    for copy in up_copies.values():
        pl.when(has_down)(copy.wait_send)


def give_back(shards, heads, out, grad_q, part_k, part_v, cosine, sine):
    tokens, narrow = part_k.shape[1:]
    rows = tokens // heads
    low = jnp.bfloat16
    vmem = pl.BlockSpec(memory_space=pltpu.VMEM)
    hbm = pl.BlockSpec(memory_space=pl.ANY)
    wide_out = jax.ShapeDtypeStruct((rows, out.shape[1] * heads), low)
    narrow_out = jax.ShapeDtypeStruct((rows, narrow * heads), low)
    return pl.pallas_call(
        functools.partial(return_kernel, shards, heads),
        out_shape=[wide_out, wide_out, narrow_out, narrow_out],
        in_specs=[hbm, hbm, vmem, vmem, vmem, vmem],
        out_specs=[hbm] * 4,
        scratch_shapes=[
            pltpu.VMEM((2, 5, tokens, narrow), low),
            pltpu.VMEM((2, 4, tokens, narrow), low),
            pltpu.VMEM((2, 2, tokens, narrow), low),
            pltpu.VMEM((2, 2, tokens, narrow), low),
            pltpu.VMEM((2, tokens, narrow), low),
            pltpu.SemaphoreType.DMA((4, heads - 1)),
            pltpu.SemaphoreType.DMA((4, heads - 1)),
            pltpu.SemaphoreType.DMA((4,)),
            pltpu.SemaphoreType.DMA((2, 8)),
            pltpu.SemaphoreType.DMA((2, 8)),
        ],
        compiler_params=pltpu.CompilerParams(
            collective_id=1, has_side_effects=True, vmem_limit_bytes=VMEM_LIMIT
        ),
        name="give_back",
    )(out, grad_q, part_k, part_v, cosine, sine)


def run(shards, heads, queries, keys, values, grad_attn, parent_gap):
    tokens = queries.shape[0] * heads
    levels = WINDOW // tokens
    assert levels * FORK == SLOTS - 1 and shards % 4 == 0
    own_shard = lax.axis_index("ctx")
    depth, slot, present = tree_tables(parent_gap, own_shard, levels)
    cosine, sine = angles(depth, tokens)
    table = jnp.concatenate([slot, present])
    qh, gh, kb, vb = gather(
        shards, heads, queries, keys, values, grad_attn, cosine, sine
    )
    out, grad_q, part_k, part_v = attend(levels, table, qh, gh, kb, vb, cosine, sine)
    return tuple(give_back(shards, heads, out, grad_q, part_k, part_v, cosine, sine))


def solution(mesh):
    rows = P(("ctx", "head"), None)
    return jax.shard_map(
        functools.partial(run, mesh.shape["ctx"], mesh.shape["head"]),
        mesh=mesh,
        in_specs=(rows, rows, rows, rows, P()),
        out_specs=(rows, rows, rows, rows),
        check_vma=False,
    )
```

```python
import functools
import math

import jax
import jax.numpy as jnp
from jax import lax
from jax.experimental import pallas as pl
from jax.experimental.pallas import tpu as pltpu
from jax.sharding import PartitionSpec as P

HD = 256
GROUP = 2
WINDOW = 1024
FORK = 2
BASE = 10000.0
SLOTS = 9
VMEM_LIMIT = 60 * 2**20
MESH = pl.DeviceIdType.MESH


def turn(block, cosine, sine):
    half = HD // 2
    first, second = block[:, :half], block[:, half:]
    return jnp.concatenate([first * cosine - second * sine, second * cosine + first * sine], -1)


def greet(shards, heads):
    me, head = lax.axis_index("ctx"), lax.axis_index("head")
    core, row = lax.rem(me, 2), lax.rem(me // 2, 2)
    barrier = pltpu.get_barrier_semaphore()
    up, down = me + 4 < shards, me >= 4
    for step in range(1, heads):
        pl.semaphore_signal(
            barrier, inc=1, device_id={"head": lax.rem(head + step, heads)}, device_id_type=MESH
        )
    for other in (me + 1 - 2 * core, me + 2 - 4 * row):
        pl.semaphore_signal(barrier, inc=1, device_id={"ctx": other}, device_id_type=MESH)

    @pl.when(up)
    def _():
        pl.semaphore_signal(barrier, inc=1, device_id={"ctx": me + 4}, device_id_type=MESH)

    @pl.when(down)
    def _():
        pl.semaphore_signal(barrier, inc=1, device_id={"ctx": me - 4}, device_id_type=MESH)

    pl.semaphore_wait(barrier, heads + 1 + up.astype(jnp.int32) + down.astype(jnp.int32))
    return me, head, core, row


def both(*terms):
    return functools.reduce(jnp.logical_and, terms)


def remote(src, dst, send_sem, recv_sem, device):
    return pltpu.make_async_remote_copy(
        src_ref=src,
        dst_ref=dst,
        send_sem=send_sem,
        recv_sem=recv_sem,
        device_id=device,
        device_id_type=MESH,
    )


def gather_kernel(
    shards, heads, levels, gap, q, k, v, g, qh, gh, kb, vb, table, cosine, sine,
    qi, ki, qr, kr, i_sem, y_send, y_recv, y_local, c_send, c_recv,
):
    load_k = pltpu.make_async_copy(k, ki, i_sem.at[0])
    load_q = pltpu.make_async_copy(q, qi, i_sem.at[1])
    load_k.start()
    load_q.start()
    me, head, core, row = greet(shards, heads)
    rows = q.shape[0]
    tokens = rows * heads

    def group(step):
        return pl.ds(pl.multiple_of(lax.rem(head + step, heads) * rows, rows), rows)

    def own_columns(src):
        width = src.shape[1] // heads
        return src.at[:, pl.ds(pl.multiple_of(head * width, width), width)]

    mine = group(0)
    exchanged = {}

    def exchange(index, src, dst):
        width = src.shape[1] // heads
        copies = []
        for step in range(1, heads):
            peer = lax.rem(head + step, heads)
            columns = pl.ds(pl.multiple_of(peer * width, width), width)
            copies.append(
                remote(
                    src.at[:, columns], dst.at[mine, :],
                    y_send.at[index, step - 1], y_recv.at[index, step - 1], {"head": peer},
                )
            )
        local = pltpu.make_async_copy(own_columns(src), dst.at[mine, :], y_local.at[index])
        for copy in copies:
            copy.start()
        local.start()
        exchanged[index] = (copies, local)

    buffers = (kb, vb)
    sends = []

    def send(chunk, src, dst, target, *conditions, source=None):
        kv, step = chunk
        at = group(step)
        copy = remote(
            buffers[kv].at[src, at, :] if source is None else own_columns(source),
            buffers[kv].at[dst, at, :],
            c_send.at[len(sends)], c_recv.at[kv, step, dst], {"ctx": target},
        )
        condition = both(me >= src, *conditions)
        pl.when(condition)(copy.start)
        sends.append((condition, copy))

    def received(chunk, slot):
        kv, step = chunk
        place = buffers[kv].at[slot, group(step), :]
        copy = remote(
            place, place, c_send.at[0], c_recv.at[kv, step, slot], {"ctx": me + 1 - 2 * core}
        )
        pl.when(me >= slot)(copy.wait_recv)

    up = me + 4 < shards

    def first(chunk, source=None):
        send(chunk, 0, 4, me + 4, up, source=source)
        send(chunk, 0, 2, me + 2, row == 0, source=source)
        send(chunk, 0, 1, me + 1, core == 0, source=source)

    first((1, 0), v)
    exchange(1, v, vb.at[0])

    def count(i, depth):
        return depth + jnp.where(jnp.logical_and(i <= me, gap[i] == 1), 1, 0)

    depth = lax.fori_loop(0, shards, count, jnp.int32(0))
    height = jnp.int32(0)
    slots = [jnp.int32(0)] * (levels + 1)
    for offset in range(1, SLOTS):
        height = height + jnp.where(gap[jnp.maximum(me - offset + 1, 0)] == 1, 1, 0)
        for j in range(1, levels + 1):
            found = both(slots[j] == 0, height == j, me >= offset)
            slots[j] = jnp.where(found, offset, slots[j])
    for j in range(levels + 1):
        table[j] = slots[j]
        table[levels + 1 + j] = jnp.int32(1) if j == 0 else jnp.where(slots[j] > 0, 1, 0)

    half = HD // 2
    position = depth * tokens + lax.broadcasted_iota(jnp.int32, (tokens, half), 0)
    lane = lax.broadcasted_iota(jnp.int32, (tokens, half), 1).astype(jnp.float32)
    angle = position.astype(jnp.float32) * jnp.exp(lane * (-2.0 * math.log(BASE) / HD))
    cosine[...] = jnp.cos(angle)
    sine[...] = jnp.sin(angle)
    cos, sin = cosine[mine, :], sine[mine, :]

    def rotate(src, dst):
        for i in range(src.shape[1] // HD):
            at = slice(i * HD, (i + 1) * HD)
            dst[:, at] = turn(src[:, at].astype(jnp.float32), cos, sin).astype(jnp.bfloat16)

    load_k.wait()
    rotate(ki, kr)
    exchange(0, kr, kb.at[0])
    first((0, 0), kr)
    load_q.wait()
    rotate(qi, qr)
    for step in range(1, heads):
        for kv in (1, 0):
            exchanged[kv][0][heads - step - 1].wait_recv()
            first((kv, step))
    exchange(2, qr, qh)
    exchange(3, g, gh)

    def second(chunk):
        received(chunk, 4)
        send(chunk, 4, 8, me + 4, up)
        send(chunk, 4, 6, me + 2, row == 0)
        send(chunk, 4, 2, me - 2, row == 1)
        send(chunk, 4, 5, me + 1, core == 0)
        send(chunk, 4, 3, me - 1, core == 1)

    def across(chunk):
        received(chunk, 2)
        send(chunk, 2, 3, me + 1, core == 0)
        send(chunk, 2, 1, me - 1, core == 1)

    def third(chunk):
        received(chunk, 8)
        send(chunk, 8, 6, me - 2, row == 1)
        send(chunk, 8, 7, me - 1, core == 1)

    def last(chunk):
        received(chunk, 6)
        send(chunk, 6, 7, me + 1, core == 0)
        send(chunk, 6, 5, me - 1, core == 1)

    chunks = [(kv, step) for step in range(heads) for kv in (1, 0)]
    for ahead, behind in ((second, across), (third, last)):
        for chunk, before in zip(chunks + [None], [None] + chunks):
            if chunk is not None:
                ahead(chunk)
            if before is not None:
                behind(before)
    for index in range(4):
        copies, local = exchanged[index]
        local.wait()
        for copy in copies:
            copy.wait_send()
            if index > 1:
                copy.wait_recv()
    for slot in (1, 3, 5, 7):
        for chunk in chunks:
            received(chunk, slot)
    for condition, copy in sends:
        pl.when(condition)(copy.wait_send)


def gather(shards, heads, levels, gap, q, k, v, g):
    rows = q.shape[0]
    tokens = rows * heads
    wide, narrow = q.shape[1] // heads, k.shape[1] // heads
    vmem = pl.BlockSpec(memory_space=pltpu.VMEM)
    smem = pl.BlockSpec(memory_space=pltpu.SMEM)
    hbm = pl.BlockSpec(memory_space=pltpu.HBM)
    low = jnp.bfloat16
    angle = jax.ShapeDtypeStruct((tokens, HD // 2), jnp.float32)
    return pl.pallas_call(
        functools.partial(gather_kernel, shards, heads, levels),
        out_shape=[
            jax.ShapeDtypeStruct((tokens, wide), low),
            jax.ShapeDtypeStruct((tokens, wide), low),
            jax.ShapeDtypeStruct((SLOTS, tokens, narrow), low),
            jax.ShapeDtypeStruct((SLOTS, tokens, narrow), low),
            jax.ShapeDtypeStruct((2 * (levels + 1),), jnp.int32),
            angle,
            angle,
        ],
        in_specs=[smem] + [hbm] * 4,
        out_specs=[hbm] * 4 + [smem, vmem, vmem],
        scratch_shapes=[
            pltpu.VMEM(q.shape, low),
            pltpu.VMEM(k.shape, low),
            pltpu.VMEM(q.shape, low),
            pltpu.VMEM(k.shape, low),
            pltpu.SemaphoreType.DMA((2,)),
            pltpu.SemaphoreType.DMA((4, heads - 1)),
            pltpu.SemaphoreType.DMA((4, heads - 1)),
            pltpu.SemaphoreType.DMA((4,)),
            pltpu.SemaphoreType.DMA((28 * heads,)),
            pltpu.SemaphoreType.DMA((2, heads, SLOTS)),
        ],
        compiler_params=pltpu.CompilerParams(
            collective_id=0, has_side_effects=True, vmem_limit_bytes=VMEM_LIMIT
        ),
        name="gather",
    )(gap, q, k, v, g)


def attend_kernel(levels, table, *refs):
    q, g = refs[:2]
    keys, values = refs[2 : 3 + levels], refs[3 + levels : 4 + 2 * levels]
    cosine, sine, out, grad_q, part_k, part_v = refs[4 + 2 * levels :]
    tokens = q.shape[0]
    scaling = HD**-0.5
    f32, low = jnp.float32, jnp.bfloat16
    query = jnp.concatenate([q[:, i * HD : (i + 1) * HD] for i in range(GROUP)], 0)
    grad = jnp.concatenate([g[:, i * HD : (i + 1) * HD] for i in range(GROUP)], 0)
    across = (((1,), (1,)), ((), ()))
    down = (((0,), (0,)), ((), ()))
    key_at = lax.broadcasted_iota(jnp.int32, (tokens, tokens), 1)
    query_at = lax.broadcasted_iota(jnp.int32, (tokens, tokens), 0)
    later = jnp.concatenate([(key_at - query_at).astype(f32)] * GROUP, 0) > 0
    scores = []
    for j in range(levels + 1):
        s = lax.dot_general(query, keys[j][0], across, preferred_element_type=f32) * scaling
        if j == 0:
            s = jnp.where(later, -1e30, s)
        else:
            if j == levels:
                s = jnp.where(later, s, -1e30)
            s = jnp.where(table[levels + 1 + j] > 0, s, -1e30)
        scores.append(s)
    highest = functools.reduce(jnp.maximum, [jnp.max(s, -1, keepdims=True) for s in scores])
    raw = [jnp.exp(s - highest) for s in scores]
    total = sum(jnp.sum(r, -1, keepdims=True) for r in raw)
    inverse = 1.0 / total
    probs = [r * inverse for r in raw]
    probs_low = [p.astype(low) for p in probs]
    attended = sum(
        lax.dot(p, values[j][0], preferred_element_type=f32) for j, p in enumerate(probs_low)
    )
    grad_probs = [
        lax.dot_general(grad, values[j][0], across, preferred_element_type=f32)
        for j in range(levels + 1)
    ]
    delta = sum(jnp.sum(p * d, -1, keepdims=True) for p, d in zip(probs, grad_probs))
    grad_scores = [
        (p * (d - delta) * scaling).astype(low) for p, d in zip(probs, grad_probs)
    ]
    turned = sum(
        lax.dot(d, keys[j][0], preferred_element_type=f32) for j, d in enumerate(grad_scores)
    )
    cos, sin = cosine[...], -sine[...]
    for i in range(GROUP):
        rows, at = slice(i * tokens, (i + 1) * tokens), slice(i * HD, (i + 1) * HD)
        out[:, at] = attended[rows].astype(low)
        grad_q[:, at] = turn(turned[rows], cos, sin).astype(low)
    part_k[...] = jnp.zeros_like(part_k)
    part_v[...] = jnp.zeros_like(part_v)
    for j in range(levels + 1):

        def put(j=j):
            slot = table[j]
            part_k[slot] = lax.dot_general(
                grad_scores[j], query, down, preferred_element_type=f32
            ).astype(low)
            part_v[slot] = lax.dot_general(
                probs_low[j], grad, down, preferred_element_type=f32
            ).astype(low)

        pl.when(table[levels + 1 + j] > 0)(put)


def attend(levels, table, qh, gh, kb, vb, cosine, sine):
    tokens = qh.shape[0]
    kv_local = kb.shape[2] // HD
    low = jnp.bfloat16

    def chosen(j):
        return pl.BlockSpec((1, tokens, HD), lambda h, t: (t[j], 0, h))

    wide = pl.BlockSpec((tokens, GROUP * HD), lambda h, t: (0, h))
    table_spec = pl.BlockSpec((tokens, HD // 2), lambda h, t: (0, 0))
    part = pl.BlockSpec((SLOTS, tokens, HD), lambda h, t: (0, 0, h))
    count = levels + 1
    return pl.pallas_call(
        functools.partial(attend_kernel, levels),
        out_shape=[
            jax.ShapeDtypeStruct(qh.shape, low),
            jax.ShapeDtypeStruct(qh.shape, low),
            jax.ShapeDtypeStruct(kb.shape, low),
            jax.ShapeDtypeStruct(vb.shape, low),
        ],
        grid_spec=pltpu.PrefetchScalarGridSpec(
            num_scalar_prefetch=1,
            grid=(kv_local,),
            in_specs=[wide, wide]
            + [chosen(j) for j in range(count)] * 2
            + [table_spec, table_spec],
            out_specs=[wide, wide, part, part],
        ),
        compiler_params=pltpu.CompilerParams(vmem_limit_bytes=VMEM_LIMIT),
        name="attend",
    )(table, qh, gh, *[kb] * count, *[vb] * count, cosine, sine)


def return_kernel(
    shards, heads, out, grad_q, part_k, part_v, cosine, sine, out_o, out_q, out_k, out_v,
    acc, from_core, from_row, from_up, done, a_sem, y_send, y_recv, y_local,
    p_send, p_recv, p_local, c_send, c_recv,
):
    parts = (part_k, part_v)
    loads = {}
    for at in (3, 4, 1, 2, 0):
        for kv in (0, 1):
            loads[kv, at] = pltpu.make_async_copy(
                parts[kv].at[2 * at], acc.at[kv, at], a_sem.at[kv, at]
            )
            loads[kv, at].start()
    me, head, core, row = greet(shards, heads)
    rows = out_o.shape[0]
    f32, low = jnp.float32, jnp.bfloat16
    exchanged = []

    def group(step):
        return pl.ds(pl.multiple_of(lax.rem(head + 1 + step, heads) * rows, rows), rows)

    def exchange(src, dst):
        index = len(exchanged)
        width = src.shape[1]
        columns = pl.ds(pl.multiple_of(head * width, width), width)
        copies = []
        for step in range(1, heads):
            peer = lax.rem(head + step, heads)
            copies.append(
                remote(
                    src.at[group(step - 1), :], dst.at[:, columns],
                    y_send.at[index, step - 1], y_recv.at[index, step - 1], {"head": peer},
                )
            )
        local = pltpu.make_async_copy(
            src.at[group(heads - 1), :], dst.at[:, columns], y_local.at[index]
        )
        for copy in copies:
            copy.start()
        local.start()
        exchanged.append((copies, local))

    chunks = [(kv, step) for step in range(heads) for kv in (0, 1)]
    core_copies, row_copies, down_copies = {}, {}, {}
    for pair in ((3, 2), (1, 0)):
        for kv, step in chunks:
            at = group(step)
            for i in pair:
                core_copies[kv, step, i] = remote(
                    parts[kv].at[2 * i + 1, at, :], from_core.at[kv, i, at, :],
                    c_send.at[kv, step, i], c_recv.at[kv, step, i],
                    {"ctx": me + 1 - 2 * core},
                )
                core_copies[kv, step, i].start()

    def to_row(chunk, i, slot):
        kv, step = chunk
        at = group(step)
        row_copies[kv, step, i] = remote(
            acc.at[kv, slot // 2, at, :], from_row.at[kv, i, at, :],
            c_send.at[kv, step, 4 + i], c_recv.at[kv, step, 4 + i],
            {"ctx": me + 2 - 4 * row},
        )
        row_copies[kv, step, i].start()

    has_down, has_up = me >= 4, me + 4 < shards

    def to_down(chunk, i, slot):
        kv, step = chunk
        at = group(step)
        down_copies[kv, step, i] = remote(
            acc.at[kv, slot // 2, at, :], from_up.at[kv, i, at, :],
            c_send.at[kv, step, 6 + i], c_recv.at[kv, step, 6 + i], {"ctx": me - 4},
        )
        pl.when(has_down)(down_copies[kv, step, i].start)

    def add(chunk, slot, pieces, i):
        kv, step = chunk
        at = group(step)
        total = acc[kv, slot // 2, at, :].astype(f32) + pieces[kv, i, at, :].astype(f32)
        acc[kv, slot // 2, at, :] = total.astype(low)

    def add_when(condition, *args):
        pl.when(condition)(lambda: add(*args))

    for copy in loads.values():
        copy.wait()
    for chunk in chunks:
        core_copies[*chunk, 3].wait_recv()
        core_copies[*chunk, 2].wait_recv()
        add(chunk, 6, from_core, 3 - core)
        to_row(chunk, 1, 6)
        add_when(core == 1, chunk, 8, from_core, 3)
    exchange(out, out_o)
    exchange(grad_q, out_q)
    for chunk in chunks:
        core_copies[*chunk, 1].wait_recv()
        core_copies[*chunk, 0].wait_recv()
        add(chunk, 2, from_core, 1 - core)
        to_row(chunk, 0, 2)
        add(chunk, 4, from_core, 2 - core)
        add_when(core == 0, chunk, 0, from_core, 0)
    for chunk in chunks:
        row_copies[*chunk, 1].wait_recv()
        add_when(row == 1, chunk, 8, from_row, 1)
        to_down(chunk, 1, 8)
        add_when(row == 0, chunk, 4, from_row, 1)

    def middle(chunk):
        row_copies[*chunk, 0].wait_recv()
        add_when(row == 1, chunk, 4, from_row, 0)
        add_when(row == 0, chunk, 0, from_row, 0)

        @pl.when(has_up)
        def _():
            down_copies[*chunk, 1].wait_recv()
            add(chunk, 4, from_up, 1)

        to_down(chunk, 0, 4)

    finals = []

    def final(chunk):
        kv, step = chunk
        at = group(step)

        @pl.when(has_up)
        def _():
            down_copies[*chunk, 0].wait_recv()
            add(chunk, 0, from_up, 0)

        if kv == 0:
            cos, sin = cosine[at, :], -sine[at, :]
            for i in range(acc.shape[3] // HD):
                col = slice(i * HD, (i + 1) * HD)
                done[kv, at, col] = turn(acc[kv, 0, at, col].astype(f32), cos, sin).astype(low)
        else:
            done[kv, at, :] = acc[kv, 0, at, :]
        width = acc.shape[3]
        dst = (out_k, out_v)[kv].at[:, pl.ds(pl.multiple_of(head * width, width), width)]
        if step == heads - 1:
            copy = pltpu.make_async_copy(done.at[kv, at, :], dst, p_local.at[kv])
        else:
            copy = remote(
                done.at[kv, at, :], dst, p_send.at[kv, step], p_recv.at[kv, step],
                {"head": lax.rem(head + 1 + step, heads)},
            )
        copy.start()
        finals.append(copy)

    for chunk, before in zip(chunks + [None], [None] + chunks):
        if chunk is not None:
            middle(chunk)
        if before is not None:
            final(before)
    for copies, local in exchanged:
        for copy in copies:
            copy.wait()
        local.wait()
    for copies in (core_copies, row_copies):
        for copy in copies.values():
            copy.wait_send()
    for copy in down_copies.values():
        pl.when(has_down)(copy.wait_send)
    for copy in finals:
        copy.wait()


def give_back(shards, heads, out, grad_q, part_k, part_v, cosine, sine):
    tokens, narrow = part_k.shape[1:]
    rows = tokens // heads
    low = jnp.bfloat16
    vmem = pl.BlockSpec(memory_space=pltpu.VMEM)
    hbm = pl.BlockSpec(memory_space=pltpu.HBM)
    wide_out = jax.ShapeDtypeStruct((rows, out.shape[1] * heads), low)
    narrow_out = jax.ShapeDtypeStruct((rows, narrow * heads), low)
    peers = heads - 1
    return pl.pallas_call(
        functools.partial(return_kernel, shards, heads),
        out_shape=[wide_out, wide_out, narrow_out, narrow_out],
        in_specs=[hbm, hbm, hbm, hbm, vmem, vmem],
        out_specs=[pl.BlockSpec(memory_space=pl.ANY)] * 4,
        scratch_shapes=[
            pltpu.VMEM((2, 5, tokens, narrow), low),
            pltpu.VMEM((2, 4, tokens, narrow), low),
            pltpu.VMEM((2, 2, tokens, narrow), low),
            pltpu.VMEM((2, 2, tokens, narrow), low),
            pltpu.VMEM((2, tokens, narrow), low),
            pltpu.SemaphoreType.DMA((2, 5)),
            pltpu.SemaphoreType.DMA((2, peers)),
            pltpu.SemaphoreType.DMA((2, peers)),
            pltpu.SemaphoreType.DMA((2,)),
            pltpu.SemaphoreType.DMA((2, peers)),
            pltpu.SemaphoreType.DMA((2, peers)),
            pltpu.SemaphoreType.DMA((2,)),
            pltpu.SemaphoreType.DMA((2, heads, 8)),
            pltpu.SemaphoreType.DMA((2, heads, 8)),
        ],
        compiler_params=pltpu.CompilerParams(
            collective_id=1, has_side_effects=True, vmem_limit_bytes=VMEM_LIMIT
        ),
        name="give_back",
    )(out, grad_q, part_k, part_v, cosine, sine)


def settle_kernel(*refs):
    count = len(refs) // 2
    copies = [
        pltpu.make_async_copy(refs[i], refs[count + i], refs[-1].at[i]) for i in range(count)
    ]
    for copy in copies:
        copy.start()
    for copy in copies:
        copy.wait()


def settle(*arrays):
    space = pl.BlockSpec(memory_space=pl.ANY)
    return pl.pallas_call(
        settle_kernel,
        out_shape=[jax.ShapeDtypeStruct(a.shape, a.dtype) for a in arrays],
        in_specs=[space] * len(arrays),
        out_specs=[pl.BlockSpec(memory_space=pltpu.HBM)] * len(arrays),
        scratch_shapes=[pltpu.SemaphoreType.DMA((len(arrays),))],
        name="settle",
    )(*arrays)


def run(shards, heads, queries, keys, values, grad_attn, parent_gap):
    tokens = queries.shape[0] * heads
    levels = WINDOW // tokens
    assert levels * FORK == SLOTS - 1 and shards % 4 == 0
    qh, gh, kb, vb, table, cosine, sine = gather(
        shards, heads, levels, parent_gap, queries, keys, values, grad_attn
    )
    out, grad_q, part_k, part_v = attend(levels, table, qh, gh, kb, vb, cosine, sine)
    return tuple(settle(*give_back(shards, heads, out, grad_q, part_k, part_v, cosine, sine)))


def solution(mesh):
    rows = P(("ctx", "head"), None)
    return jax.shard_map(
        functools.partial(run, mesh.shape["ctx"], mesh.shape["head"]),
        mesh=mesh,
        in_specs=(rows, rows, rows, rows, P()),
        out_specs=(rows, rows, rows, rows),
        check_vma=False,
    )
```

```python
import functools
import math

import jax
import jax.numpy as jnp
from jax import lax
from jax.experimental import pallas as pl
from jax.experimental.pallas import tpu as pltpu
from jax.sharding import PartitionSpec as P

HD = 256
GROUP = 2
WINDOW = 1024
FORK = 2
BASE = 10000.0
SLOTS = 9
VMEM_LIMIT = 60 * 2**20
MESH = pl.DeviceIdType.MESH


def turn(block, cosine, sine):
    half = HD // 2
    first, second = block[:, :half], block[:, half:]
    return jnp.concatenate([first * cosine - second * sine, second * cosine + first * sine], -1)


def greet(shards, heads):
    me, head = lax.axis_index("ctx"), lax.axis_index("head")
    core, row = lax.rem(me, 2), lax.rem(me // 2, 2)
    barrier = pltpu.get_barrier_semaphore()
    up, down = me + 4 < shards, me >= 4
    for step in range(1, heads):
        pl.semaphore_signal(
            barrier, inc=1, device_id={"head": lax.rem(head + step, heads)}, device_id_type=MESH
        )
    for other in (me + 1 - 2 * core, me + 2 - 4 * row):
        pl.semaphore_signal(barrier, inc=1, device_id={"ctx": other}, device_id_type=MESH)

    @pl.when(up)
    def _():
        pl.semaphore_signal(barrier, inc=1, device_id={"ctx": me + 4}, device_id_type=MESH)

    @pl.when(down)
    def _():
        pl.semaphore_signal(barrier, inc=1, device_id={"ctx": me - 4}, device_id_type=MESH)

    pl.semaphore_wait(barrier, heads + 1 + up.astype(jnp.int32) + down.astype(jnp.int32))
    return me, head, core, row


def both(*terms):
    return functools.reduce(jnp.logical_and, terms)


def remote(src, dst, send_sem, recv_sem, device):
    return pltpu.make_async_remote_copy(
        src_ref=src,
        dst_ref=dst,
        send_sem=send_sem,
        recv_sem=recv_sem,
        device_id=device,
        device_id_type=MESH,
    )


def gather_kernel(
    shards, heads, levels, gap, q, k, v, g, qh, gh, kb_out, vb_out, table, cosine, sine,
    qi, ki, vi, gi, qr, kr, kb, vb, i_sem, o_sem, y_send, y_recv, y_local, c_send, c_recv,
):
    loads = [
        pltpu.make_async_copy(src, dst, i_sem.at[i])
        for i, (src, dst) in enumerate(((k, ki), (v, vi), (q, qi), (g, gi)))
    ]
    for i in (1, 0, 2, 3):
        loads[i].start()
    me, head, core, row = greet(shards, heads)
    rows = q.shape[0]
    tokens = rows * heads

    def group(step):
        return pl.ds(pl.multiple_of(lax.rem(head + step, heads) * rows, rows), rows)

    def own_columns(src):
        width = src.shape[1] // heads
        return src.at[:, pl.ds(pl.multiple_of(head * width, width), width)]

    mine = group(0)
    exchanged = {}

    def exchange(index, src, dst):
        width = src.shape[1] // heads
        copies = []
        for step in range(1, heads):
            peer = lax.rem(head + step, heads)
            columns = pl.ds(pl.multiple_of(peer * width, width), width)
            copies.append(
                remote(
                    src.at[:, columns], dst.at[mine, :],
                    y_send.at[index, step - 1], y_recv.at[index, step - 1], {"head": peer},
                )
            )
        local = pltpu.make_async_copy(own_columns(src), dst.at[mine, :], y_local.at[index])
        for copy in copies:
            copy.start()
        local.start()
        exchanged[index] = (copies, local)

    buffers, outputs = (kb, vb), (kb_out, vb_out)
    sends, stores = [], []

    def store(chunk, slot):
        kv, step = chunk
        at = group(step)
        copy = pltpu.make_async_copy(
            buffers[kv].at[slot, at, :], outputs[kv].at[slot, at, :], o_sem.at[kv, step, slot]
        )
        pl.when(me >= slot)(copy.start)
        stores.append((me >= slot, copy))

    def send(chunk, src, dst, target, *conditions, source=None):
        kv, step = chunk
        at = group(step)
        copy = remote(
            buffers[kv].at[src, at, :] if source is None else own_columns(source),
            buffers[kv].at[dst, at, :],
            c_send.at[len(sends)], c_recv.at[kv, step, dst], {"ctx": target},
        )
        condition = both(me >= src, *conditions)
        pl.when(condition)(copy.start)
        sends.append((condition, copy))

    def received(chunk, slot):
        kv, step = chunk
        place = buffers[kv].at[slot, group(step), :]
        copy = remote(
            place, place, c_send.at[0], c_recv.at[kv, step, slot], {"ctx": me + 1 - 2 * core}
        )
        pl.when(me >= slot)(copy.wait_recv)
        store(chunk, slot)

    up = me + 4 < shards

    def first(chunk, source=None):
        send(chunk, 0, 4, me + 4, up, source=source)
        send(chunk, 0, 2, me + 2, row == 0, source=source)
        send(chunk, 0, 1, me + 1, core == 0, source=source)

    loads[1].wait()
    first((1, 0), vi)
    exchange(1, vi, vb.at[0])

    def count(i, depth):
        return depth + jnp.where(jnp.logical_and(i <= me, gap[i] == 1), 1, 0)

    depth = lax.fori_loop(0, shards, count, jnp.int32(0))
    height = jnp.int32(0)
    slots = [jnp.int32(0)] * (levels + 1)
    for offset in range(1, SLOTS):
        height = height + jnp.where(gap[jnp.maximum(me - offset + 1, 0)] == 1, 1, 0)
        for j in range(1, levels + 1):
            found = both(slots[j] == 0, height == j, me >= offset)
            slots[j] = jnp.where(found, offset, slots[j])
    for j in range(levels + 1):
        table[j] = slots[j]
        table[levels + 1 + j] = jnp.int32(1) if j == 0 else jnp.where(slots[j] > 0, 1, 0)

    half = HD // 2
    position = depth * tokens + lax.broadcasted_iota(jnp.int32, (tokens, half), 0)
    lane = lax.broadcasted_iota(jnp.int32, (tokens, half), 1).astype(jnp.float32)
    angle = position.astype(jnp.float32) * jnp.exp(lane * (-2.0 * math.log(BASE) / HD))
    cosine[...] = jnp.cos(angle)
    sine[...] = jnp.sin(angle)
    cos, sin = cosine[mine, :], sine[mine, :]

    def rotate(src, dst):
        for i in range(src.shape[1] // HD):
            at = slice(i * HD, (i + 1) * HD)
            dst[:, at] = turn(src[:, at].astype(jnp.float32), cos, sin).astype(jnp.bfloat16)

    loads[0].wait()
    rotate(ki, kr)
    exchange(0, kr, kb.at[0])
    first((0, 0), kr)
    loads[2].wait()
    rotate(qi, qr)
    for step in range(1, heads):
        for kv in (1, 0):
            exchanged[kv][0][heads - step - 1].wait_recv()
            first((kv, step))
            store((kv, step), 0)
    exchange(2, qr, qh)
    loads[3].wait()
    exchange(3, gi, gh)
    for kv in (1, 0):
        exchanged[kv][1].wait()
        store((kv, 0), 0)

    def second(chunk):
        received(chunk, 4)
        send(chunk, 4, 8, me + 4, up)
        send(chunk, 4, 6, me + 2, row == 0)
        send(chunk, 4, 2, me - 2, row == 1)
        send(chunk, 4, 5, me + 1, core == 0)
        send(chunk, 4, 3, me - 1, core == 1)

    def across(chunk):
        received(chunk, 2)
        send(chunk, 2, 3, me + 1, core == 0)
        send(chunk, 2, 1, me - 1, core == 1)

    def third(chunk):
        received(chunk, 8)
        send(chunk, 8, 6, me - 2, row == 1)
        send(chunk, 8, 7, me - 1, core == 1)

    def last(chunk):
        received(chunk, 6)
        send(chunk, 6, 7, me + 1, core == 0)
        send(chunk, 6, 5, me - 1, core == 1)

    chunks = [(kv, step) for step in range(heads) for kv in (1, 0)]
    for ahead, behind in ((second, across), (third, last)):
        for chunk, before in zip(chunks + [None], [None] + chunks):
            if chunk is not None:
                ahead(chunk)
            if before is not None:
                behind(before)
    for index in range(4):
        copies, local = exchanged[index]
        if index > 1:
            local.wait()
        for copy in copies:
            copy.wait_send()
            if index > 1:
                copy.wait_recv()
    for slot in (1, 3, 5, 7):
        for chunk in chunks:
            received(chunk, slot)
    for condition, copy in sends:
        pl.when(condition)(copy.wait_send)
    for condition, copy in stores:
        pl.when(condition)(copy.wait)


def gather(shards, heads, levels, gap, q, k, v, g):
    rows = q.shape[0]
    tokens = rows * heads
    wide, narrow = q.shape[1] // heads, k.shape[1] // heads
    vmem = pl.BlockSpec(memory_space=pltpu.VMEM)
    smem = pl.BlockSpec(memory_space=pltpu.SMEM)
    hbm = pl.BlockSpec(memory_space=pltpu.HBM)
    low = jnp.bfloat16
    angle = jax.ShapeDtypeStruct((tokens, HD // 2), jnp.float32)
    return pl.pallas_call(
        functools.partial(gather_kernel, shards, heads, levels),
        out_shape=[
            jax.ShapeDtypeStruct((tokens, wide), low),
            jax.ShapeDtypeStruct((tokens, wide), low),
            jax.ShapeDtypeStruct((SLOTS, tokens, narrow), low),
            jax.ShapeDtypeStruct((SLOTS, tokens, narrow), low),
            jax.ShapeDtypeStruct((2 * (levels + 1),), jnp.int32),
            angle,
            angle,
        ],
        in_specs=[smem] + [hbm] * 4,
        out_specs=[vmem, vmem, hbm, hbm, smem, vmem, vmem],
        scratch_shapes=[
            pltpu.VMEM(q.shape, low),
            pltpu.VMEM(k.shape, low),
            pltpu.VMEM(v.shape, low),
            pltpu.VMEM(g.shape, low),
            pltpu.VMEM(q.shape, low),
            pltpu.VMEM(k.shape, low),
            pltpu.VMEM((SLOTS, tokens, narrow), low),
            pltpu.VMEM((SLOTS, tokens, narrow), low),
            pltpu.SemaphoreType.DMA((4,)),
            pltpu.SemaphoreType.DMA((2, heads, SLOTS)),
            pltpu.SemaphoreType.DMA((4, heads - 1)),
            pltpu.SemaphoreType.DMA((4, heads - 1)),
            pltpu.SemaphoreType.DMA((4,)),
            pltpu.SemaphoreType.DMA((28 * heads,)),
            pltpu.SemaphoreType.DMA((2, heads, SLOTS)),
        ],
        compiler_params=pltpu.CompilerParams(
            collective_id=0, has_side_effects=True, vmem_limit_bytes=VMEM_LIMIT
        ),
        name="gather",
    )(gap, q, k, v, g)


def attend_kernel(levels, table, *refs):
    q, g = refs[:2]
    keys, values = refs[2 : 3 + levels], refs[3 + levels : 4 + 2 * levels]
    cosine, sine, out, grad_q, part_k, part_v = refs[4 + 2 * levels :]
    tokens = q.shape[0]
    scaling = HD**-0.5
    f32, low = jnp.float32, jnp.bfloat16
    query = jnp.concatenate([q[:, i * HD : (i + 1) * HD] for i in range(GROUP)], 0)
    query = query * jnp.asarray(scaling, low)
    grad = jnp.concatenate([g[:, i * HD : (i + 1) * HD] for i in range(GROUP)], 0)
    across = (((1,), (1,)), ((), ()))
    down = (((0,), (0,)), ((), ()))
    key_at = lax.broadcasted_iota(jnp.int32, (tokens, tokens), 1)
    query_at = lax.broadcasted_iota(jnp.int32, (tokens, tokens), 0)
    later = jnp.concatenate([(key_at - query_at).astype(f32)] * GROUP, 0) > 0
    scores = []
    for j in range(levels + 1):
        s = lax.dot_general(query, keys[j][0], across, preferred_element_type=f32)
        if j == 0:
            s = jnp.where(later, -1e30, s)
        elif j == levels:
            s = jnp.where(later, s, -1e30)
        scores.append(s)
    absent = [jnp.where(table[levels + 1 + j] > 0, 0.0, 1e30) for j in range(levels + 1)]
    highest = functools.reduce(
        jnp.maximum, [jnp.max(s, -1, keepdims=True) - a for s, a in zip(scores, absent)]
    )
    raw = [jnp.exp(s - (highest + a)) for s, a in zip(scores, absent)]
    total = sum(jnp.sum(r, -1, keepdims=True) for r in raw)
    inverse = 1.0 / total
    probs = [r * inverse for r in raw]
    probs_low = [p.astype(low) for p in probs]
    attended = sum(
        lax.dot(p, values[j][0], preferred_element_type=f32) for j, p in enumerate(probs_low)
    )
    grad_probs = [
        lax.dot_general(grad, values[j][0], across, preferred_element_type=f32)
        for j in range(levels + 1)
    ]
    delta = sum(jnp.sum(p * d, -1, keepdims=True) for p, d in zip(probs, grad_probs))
    grad_scores = [
        (p * (d - delta)).astype(low) for p, d in zip(probs, grad_probs)
    ]
    turned = scaling * sum(
        lax.dot(d, keys[j][0], preferred_element_type=f32) for j, d in enumerate(grad_scores)
    )
    cos, sin = cosine[...], -sine[...]
    for i in range(GROUP):
        rows, at = slice(i * tokens, (i + 1) * tokens), slice(i * HD, (i + 1) * HD)
        out[:, at] = attended[rows].astype(low)
        grad_q[:, at] = turn(turned[rows], cos, sin).astype(low)
    part_k[...] = jnp.zeros_like(part_k)
    part_v[...] = jnp.zeros_like(part_v)
    for j in range(levels + 1):

        def put(j=j):
            slot = table[j]
            part_k[slot] = lax.dot_general(
                grad_scores[j], query, down, preferred_element_type=f32
            ).astype(low)
            part_v[slot] = lax.dot_general(
                probs_low[j], grad, down, preferred_element_type=f32
            ).astype(low)

        pl.when(table[levels + 1 + j] > 0)(put)


def attend(levels, table, qh, gh, kb, vb, cosine, sine):
    tokens = qh.shape[0]
    kv_local = kb.shape[2] // HD
    low = jnp.bfloat16

    def chosen(j):
        return pl.BlockSpec((1, tokens, HD), lambda h, t: (t[j], 0, h))

    wide = pl.BlockSpec((tokens, GROUP * HD), lambda h, t: (0, h))
    table_spec = pl.BlockSpec((tokens, HD // 2), lambda h, t: (0, 0))
    part = pl.BlockSpec((SLOTS, tokens, HD), lambda h, t: (0, 0, h))
    count = levels + 1
    return pl.pallas_call(
        functools.partial(attend_kernel, levels),
        out_shape=[
            jax.ShapeDtypeStruct(qh.shape, low),
            jax.ShapeDtypeStruct(qh.shape, low),
            jax.ShapeDtypeStruct(kb.shape, low),
            jax.ShapeDtypeStruct(vb.shape, low),
        ],
        grid_spec=pltpu.PrefetchScalarGridSpec(
            num_scalar_prefetch=1,
            grid=(kv_local,),
            in_specs=[wide, wide]
            + [chosen(j) for j in range(count)] * 2
            + [table_spec, table_spec],
            out_specs=[wide, wide, part, part],
        ),
        compiler_params=pltpu.CompilerParams(vmem_limit_bytes=VMEM_LIMIT),
        name="attend",
    )(table, qh, gh, *[kb] * count, *[vb] * count, cosine, sine)


def return_kernel(
    shards, heads, out, grad_q, part_k, part_v, cosine, sine, out_o, out_q, out_k, out_v,
    acc, odd, from_core, from_row, from_up, done, a_sem, b_sem, y_send, y_recv, y_local,
    p_send, p_recv, p_local, c_send, c_recv,
):
    parts = (part_k, part_v)
    loads, odd_loads = {}, {}
    for i in (3, 2, 1, 0):
        for kv in (0, 1):
            odd_loads[kv, i] = pltpu.make_async_copy(
                parts[kv].at[2 * i + 1], odd.at[kv, i], b_sem.at[kv, i]
            )
            odd_loads[kv, i].start()
    for at in (3, 4, 1, 2, 0):
        for kv in (0, 1):
            loads[kv, at] = pltpu.make_async_copy(
                parts[kv].at[2 * at], acc.at[kv, at], a_sem.at[kv, at]
            )
            loads[kv, at].start()
    me, head, core, row = greet(shards, heads)
    rows = out_o.shape[0]
    f32, low = jnp.float32, jnp.bfloat16
    exchanged = []

    def group(step):
        return pl.ds(pl.multiple_of(lax.rem(head + 1 + step, heads) * rows, rows), rows)

    def exchange(src, dst):
        index = len(exchanged)
        width = src.shape[1]
        columns = pl.ds(pl.multiple_of(head * width, width), width)
        copies = []
        for step in range(1, heads):
            peer = lax.rem(head + step, heads)
            copies.append(
                remote(
                    src.at[group(step - 1), :], dst.at[:, columns],
                    y_send.at[index, step - 1], y_recv.at[index, step - 1], {"head": peer},
                )
            )
        local = pltpu.make_async_copy(
            src.at[group(heads - 1), :], dst.at[:, columns], y_local.at[index]
        )
        for copy in copies:
            copy.start()
        local.start()
        exchanged.append((copies, local))

    chunks = [(kv, step) for step in range(heads) for kv in (0, 1)]
    core_copies, row_copies, down_copies = {}, {}, {}
    for pair in ((3, 2), (1, 0)):
        for kv, step in chunks:
            at = group(step)
            for i in pair:
                if step == 0:
                    odd_loads[kv, i].wait()
                core_copies[kv, step, i] = remote(
                    odd.at[kv, i, at, :], from_core.at[kv, i, at, :],
                    c_send.at[kv, step, i], c_recv.at[kv, step, i],
                    {"ctx": me + 1 - 2 * core},
                )
                core_copies[kv, step, i].start()

    def to_row(chunk, i, slot):
        kv, step = chunk
        at = group(step)
        row_copies[kv, step, i] = remote(
            acc.at[kv, slot // 2, at, :], from_row.at[kv, i, at, :],
            c_send.at[kv, step, 4 + i], c_recv.at[kv, step, 4 + i],
            {"ctx": me + 2 - 4 * row},
        )
        row_copies[kv, step, i].start()

    has_down, has_up = me >= 4, me + 4 < shards

    def to_down(chunk, i, slot):
        kv, step = chunk
        at = group(step)
        down_copies[kv, step, i] = remote(
            acc.at[kv, slot // 2, at, :], from_up.at[kv, i, at, :],
            c_send.at[kv, step, 6 + i], c_recv.at[kv, step, 6 + i], {"ctx": me - 4},
        )
        pl.when(has_down)(down_copies[kv, step, i].start)

    def add(chunk, slot, pieces, i):
        kv, step = chunk
        at = group(step)
        total = acc[kv, slot // 2, at, :].astype(f32) + pieces[kv, i, at, :].astype(f32)
        acc[kv, slot // 2, at, :] = total.astype(low)

    def add_when(condition, *args):
        pl.when(condition)(lambda: add(*args))

    for copy in loads.values():
        copy.wait()
    for chunk in chunks:
        core_copies[*chunk, 3].wait_recv()
        core_copies[*chunk, 2].wait_recv()
        add(chunk, 6, from_core, 3 - core)
        to_row(chunk, 1, 6)
        add_when(core == 1, chunk, 8, from_core, 3)
    exchange(out, out_o)
    exchange(grad_q, out_q)
    for chunk in chunks:
        core_copies[*chunk, 1].wait_recv()
        core_copies[*chunk, 0].wait_recv()
        add(chunk, 2, from_core, 1 - core)
        to_row(chunk, 0, 2)
        add(chunk, 4, from_core, 2 - core)
        add_when(core == 0, chunk, 0, from_core, 0)
    for chunk in chunks:
        row_copies[*chunk, 1].wait_recv()
        add_when(row == 1, chunk, 8, from_row, 1)
        to_down(chunk, 1, 8)
        add_when(row == 0, chunk, 4, from_row, 1)

    def middle(chunk):
        row_copies[*chunk, 0].wait_recv()
        add_when(row == 1, chunk, 4, from_row, 0)
        add_when(row == 0, chunk, 0, from_row, 0)

        @pl.when(has_up)
        def _():
            down_copies[*chunk, 1].wait_recv()
            add(chunk, 4, from_up, 1)

        to_down(chunk, 0, 4)

    finals = []

    def final(chunk):
        kv, step = chunk
        at = group(step)

        @pl.when(has_up)
        def _():
            down_copies[*chunk, 0].wait_recv()
            add(chunk, 0, from_up, 0)

        if kv == 0:
            cos, sin = cosine[at, :], -sine[at, :]
            for i in range(acc.shape[3] // HD):
                col = slice(i * HD, (i + 1) * HD)
                done[kv, at, col] = turn(acc[kv, 0, at, col].astype(f32), cos, sin).astype(low)
        else:
            done[kv, at, :] = acc[kv, 0, at, :]
        width = acc.shape[3]
        dst = (out_k, out_v)[kv].at[:, pl.ds(pl.multiple_of(head * width, width), width)]
        if step == heads - 1:
            copy = pltpu.make_async_copy(done.at[kv, at, :], dst, p_local.at[kv])
        else:
            copy = remote(
                done.at[kv, at, :], dst, p_send.at[kv, step], p_recv.at[kv, step],
                {"head": lax.rem(head + 1 + step, heads)},
            )
        copy.start()
        finals.append(copy)

    for chunk, before in zip(chunks + [None], [None] + chunks):
        if chunk is not None:
            middle(chunk)
        if before is not None:
            final(before)
    for copies, local in exchanged:
        for copy in copies:
            copy.wait()
        local.wait()
    for copies in (core_copies, row_copies):
        for copy in copies.values():
            copy.wait_send()
    for copy in down_copies.values():
        pl.when(has_down)(copy.wait_send)
    for copy in finals:
        copy.wait()


def give_back(shards, heads, out, grad_q, part_k, part_v, cosine, sine):
    tokens, narrow = part_k.shape[1:]
    rows = tokens // heads
    low = jnp.bfloat16
    vmem = pl.BlockSpec(memory_space=pltpu.VMEM)
    hbm = pl.BlockSpec(memory_space=pltpu.HBM)
    wide_out = jax.ShapeDtypeStruct((rows, out.shape[1] * heads), low)
    narrow_out = jax.ShapeDtypeStruct((rows, narrow * heads), low)
    peers = heads - 1
    return pl.pallas_call(
        functools.partial(return_kernel, shards, heads),
        out_shape=[wide_out, wide_out, narrow_out, narrow_out],
        in_specs=[vmem, vmem, hbm, hbm, vmem, vmem],
        out_specs=[vmem] * 4,
        scratch_shapes=[
            pltpu.VMEM((2, 5, tokens, narrow), low),
            pltpu.VMEM((2, 4, tokens, narrow), low),
            pltpu.VMEM((2, 4, tokens, narrow), low),
            pltpu.VMEM((2, 2, tokens, narrow), low),
            pltpu.VMEM((2, 2, tokens, narrow), low),
            pltpu.VMEM((2, tokens, narrow), low),
            pltpu.SemaphoreType.DMA((2, 5)),
            pltpu.SemaphoreType.DMA((2, 4)),
            pltpu.SemaphoreType.DMA((2, peers)),
            pltpu.SemaphoreType.DMA((2, peers)),
            pltpu.SemaphoreType.DMA((2,)),
            pltpu.SemaphoreType.DMA((2, peers)),
            pltpu.SemaphoreType.DMA((2, peers)),
            pltpu.SemaphoreType.DMA((2,)),
            pltpu.SemaphoreType.DMA((2, heads, 8)),
            pltpu.SemaphoreType.DMA((2, heads, 8)),
        ],
        compiler_params=pltpu.CompilerParams(
            collective_id=1, has_side_effects=True, vmem_limit_bytes=VMEM_LIMIT
        ),
        name="give_back",
    )(out, grad_q, part_k, part_v, cosine, sine)


def settle_kernel(count, *refs):
    given, made, held = refs[:count], refs[count : 2 * count], refs[2 * count : 3 * count]
    into, away = refs[3 * count :]
    loads = [pltpu.make_async_copy(given[i], held[i], into.at[i]) for i in range(count)]
    stores = [pltpu.make_async_copy(held[i], made[i], away.at[i]) for i in range(count)]
    for load in loads:
        load.start()
    for load, store in zip(loads, stores):
        load.wait()
        store.start()
    for store in stores:
        store.wait()


def settle(*arrays):
    count = len(arrays)
    space = pl.BlockSpec(memory_space=pltpu.HBM)
    return pl.pallas_call(
        functools.partial(settle_kernel, count),
        out_shape=[jax.ShapeDtypeStruct(a.shape, a.dtype) for a in arrays],
        in_specs=[space] * count,
        out_specs=[space] * count,
        scratch_shapes=[pltpu.VMEM(a.shape, a.dtype) for a in arrays]
        + [pltpu.SemaphoreType.DMA((count,))] * 2,
        compiler_params=pltpu.CompilerParams(vmem_limit_bytes=VMEM_LIMIT),
        name="settle",
    )(*arrays)


def run(shards, heads, queries, keys, values, grad_attn, parent_gap):
    tokens = queries.shape[0] * heads
    levels = WINDOW // tokens
    assert levels * FORK == SLOTS - 1 and shards % 4 == 0
    qh, gh, kb, vb, table, cosine, sine = gather(
        shards, heads, levels, parent_gap, queries, keys, values, grad_attn
    )
    out, grad_q, part_k, part_v = attend(levels, table, qh, gh, kb, vb, cosine, sine)
    return tuple(settle(*give_back(shards, heads, out, grad_q, part_k, part_v, cosine, sine)))


def solution(mesh):
    rows = P(("ctx", "head"), None)
    return jax.shard_map(
        functools.partial(run, mesh.shape["ctx"], mesh.shape["head"]),
        mesh=mesh,
        in_specs=(rows, rows, rows, rows, P()),
        out_specs=(rows, rows, rows, rows),
        check_vma=False,
    )
```

```python
import functools
import math

import jax
import jax.numpy as jnp
from jax import lax
from jax.experimental import pallas as pl
from jax.experimental.pallas import tpu as pltpu
from jax.sharding import PartitionSpec as P

HD = 256
GROUP = 2
WINDOW = 1024
FORK = 2
BASE = 10000.0
SLOTS = 9
SPLIT = 2
VMEM_LIMIT = 60 * 2**20
MESH = pl.DeviceIdType.MESH


def turn(block, cosine, sine):
    half = HD // 2
    first, second = block[:, :half], block[:, half:]
    return jnp.concatenate([first * cosine - second * sine, second * cosine + first * sine], -1)


def greet(shards, heads):
    me, head = lax.axis_index("ctx"), lax.axis_index("head")
    core, row = lax.rem(me, 2), lax.rem(me // 2, 2)
    barrier = pltpu.get_barrier_semaphore()
    up, down = me + 4 < shards, me >= 4
    for step in range(1, heads):
        pl.semaphore_signal(
            barrier, inc=1, device_id={"head": lax.rem(head + step, heads)}, device_id_type=MESH
        )
    for other in (me + 1 - 2 * core, me + 2 - 4 * row):
        pl.semaphore_signal(barrier, inc=1, device_id={"ctx": other}, device_id_type=MESH)

    @pl.when(up)
    def _():
        pl.semaphore_signal(barrier, inc=1, device_id={"ctx": me + 4}, device_id_type=MESH)

    @pl.when(down)
    def _():
        pl.semaphore_signal(barrier, inc=1, device_id={"ctx": me - 4}, device_id_type=MESH)

    pl.semaphore_wait(barrier, heads + 1 + up.astype(jnp.int32) + down.astype(jnp.int32))
    return me, head, core, row


def both(*terms):
    return functools.reduce(jnp.logical_and, terms)


def remote(src, dst, send_sem, recv_sem, device):
    return pltpu.make_async_remote_copy(
        src_ref=src,
        dst_ref=dst,
        send_sem=send_sem,
        recv_sem=recv_sem,
        device_id=device,
        device_id_type=MESH,
    )


def gather_kernel(
    shards, heads, levels, gap, q, k, v, g, qh, gh, kb_out, vb_out, table, cosine, sine,
    qi, ki, vi, gi, qr, kr, kb, vb, i_sem, o_sem, y_send, y_recv, y_local, c_send, c_recv,
):
    loads = [
        pltpu.make_async_copy(src, dst, i_sem.at[i])
        for i, (src, dst) in enumerate(((k, ki), (v, vi), (q, qi), (g, gi)))
    ]
    for i in (1, 0, 2, 3):
        loads[i].start()
    me, head, core, row = greet(shards, heads)
    rows = q.shape[0]
    tokens = rows * heads

    def group(step):
        return pl.ds(pl.multiple_of(lax.rem(head + step, heads) * rows, rows), rows)

    def piece(step):
        size = rows // SPLIT
        start = lax.rem(head + step // SPLIT, heads) * rows + step % SPLIT * size
        return pl.ds(pl.multiple_of(start, size), size)

    def own_columns(src, step=None):
        width = src.shape[1] // heads
        size = rows // SPLIT
        at = slice(None) if step is None else slice(step * size, (step + 1) * size)
        return src.at[at, pl.ds(pl.multiple_of(head * width, width), width)]

    mine = group(0)
    exchanged = {}

    def exchange(index, src, dst):
        width = src.shape[1] // heads
        copies = []
        for step in range(1, heads):
            peer = lax.rem(head + step, heads)
            columns = pl.ds(pl.multiple_of(peer * width, width), width)
            copies.append(
                remote(
                    src.at[:, columns], dst.at[mine, :],
                    y_send.at[index, step - 1], y_recv.at[index, step - 1], {"head": peer},
                )
            )
        local = pltpu.make_async_copy(own_columns(src), dst.at[mine, :], y_local.at[index])
        for copy in copies:
            copy.start()
        local.start()
        exchanged[index] = (copies, local)

    buffers, outputs = (kb, vb), (kb_out, vb_out)
    sends, stores = [], []

    def store(chunk, slot):
        kv, step = chunk
        at = piece(step)
        copy = pltpu.make_async_copy(
            buffers[kv].at[slot, at, :], outputs[kv].at[slot, at, :], o_sem.at[kv, step, slot]
        )
        pl.when(me >= slot)(copy.start)
        stores.append((me >= slot, copy))

    def send(chunk, src, dst, target, *conditions, source=None):
        kv, step = chunk
        at = piece(step)
        copy = remote(
            buffers[kv].at[src, at, :] if source is None else own_columns(source, step),
            buffers[kv].at[dst, at, :],
            c_send.at[len(sends)], c_recv.at[kv, step, dst], {"ctx": target},
        )
        condition = both(me >= src, *conditions)
        pl.when(condition)(copy.start)
        sends.append((condition, copy))

    def received(chunk, slot):
        kv, step = chunk
        place = buffers[kv].at[slot, piece(step), :]
        copy = remote(
            place, place, c_send.at[0], c_recv.at[kv, step, slot], {"ctx": me + 1 - 2 * core}
        )
        pl.when(me >= slot)(copy.wait_recv)
        store(chunk, slot)

    up = me + 4 < shards

    def first(chunk, source=None):
        send(chunk, 0, 4, me + 4, up, source=source)
        send(chunk, 0, 2, me + 2, row == 0, source=source)
        send(chunk, 0, 1, me + 1, core == 0, source=source)

    loads[1].wait()
    for part in range(SPLIT):
        first((1, part), vi)
    exchange(1, vi, vb.at[0])

    def count(i, depth):
        return depth + jnp.where(jnp.logical_and(i <= me, gap[i] == 1), 1, 0)

    depth = lax.fori_loop(0, shards, count, jnp.int32(0))
    height = jnp.int32(0)
    slots = [jnp.int32(0)] * (levels + 1)
    for offset in range(1, SLOTS):
        height = height + jnp.where(gap[jnp.maximum(me - offset + 1, 0)] == 1, 1, 0)
        for j in range(1, levels + 1):
            found = both(slots[j] == 0, height == j, me >= offset)
            slots[j] = jnp.where(found, offset, slots[j])
    for j in range(levels + 1):
        table[j] = slots[j]
        table[levels + 1 + j] = jnp.int32(1) if j == 0 else jnp.where(slots[j] > 0, 1, 0)

    half = HD // 2
    position = depth * tokens + lax.broadcasted_iota(jnp.int32, (tokens, half), 0)
    lane = lax.broadcasted_iota(jnp.int32, (tokens, half), 1).astype(jnp.float32)
    angle = position.astype(jnp.float32) * jnp.exp(lane * (-2.0 * math.log(BASE) / HD))
    cosine[...] = jnp.cos(angle)
    sine[...] = jnp.sin(angle)
    cos, sin = cosine[mine, :], sine[mine, :]

    def rotate(src, dst):
        for i in range(src.shape[1] // HD):
            at = slice(i * HD, (i + 1) * HD)
            dst[:, at] = turn(src[:, at].astype(jnp.float32), cos, sin).astype(jnp.bfloat16)

    loads[0].wait()
    rotate(ki, kr)
    exchange(0, kr, kb.at[0])
    for part in range(SPLIT):
        first((0, part), kr)
    loads[2].wait()
    rotate(qi, qr)
    for step in range(1, heads):
        for kv in (1, 0):
            exchanged[kv][0][heads - step - 1].wait_recv()
            for part in range(SPLIT):
                first((kv, step * SPLIT + part))
                store((kv, step * SPLIT + part), 0)
    exchange(2, qr, qh)
    loads[3].wait()
    exchange(3, gi, gh)
    for kv in (1, 0):
        exchanged[kv][1].wait()
        for part in range(SPLIT):
            store((kv, part), 0)

    def second(chunk):
        received(chunk, 4)
        send(chunk, 4, 8, me + 4, up)
        send(chunk, 4, 6, me + 2, row == 0)
        send(chunk, 4, 2, me - 2, row == 1)
        send(chunk, 4, 5, me + 1, core == 0)
        send(chunk, 4, 3, me - 1, core == 1)

    def across(chunk):
        received(chunk, 2)
        send(chunk, 2, 3, me + 1, core == 0)
        send(chunk, 2, 1, me - 1, core == 1)

    def third(chunk):
        received(chunk, 8)
        send(chunk, 8, 6, me - 2, row == 1)
        send(chunk, 8, 7, me - 1, core == 1)

    def last(chunk):
        received(chunk, 6)
        send(chunk, 6, 7, me + 1, core == 0)
        send(chunk, 6, 5, me - 1, core == 1)

    chunks = [(kv, step) for step in range(SPLIT * heads) for kv in (1, 0)]
    for ahead, behind in ((second, across), (third, last)):
        for chunk, before in zip(chunks + [None], [None] + chunks):
            if chunk is not None:
                ahead(chunk)
            if before is not None:
                behind(before)
    for index in range(4):
        copies, local = exchanged[index]
        if index > 1:
            local.wait()
        for copy in copies:
            copy.wait_send()
            if index > 1:
                copy.wait_recv()
    for slot in (1, 3, 5, 7):
        for chunk in chunks:
            received(chunk, slot)
    for condition, copy in sends:
        pl.when(condition)(copy.wait_send)
    for condition, copy in stores:
        pl.when(condition)(copy.wait)


def gather(shards, heads, levels, gap, q, k, v, g):
    rows = q.shape[0]
    tokens = rows * heads
    wide, narrow = q.shape[1] // heads, k.shape[1] // heads
    vmem = pl.BlockSpec(memory_space=pltpu.VMEM)
    smem = pl.BlockSpec(memory_space=pltpu.SMEM)
    hbm = pl.BlockSpec(memory_space=pltpu.HBM)
    low = jnp.bfloat16
    angle = jax.ShapeDtypeStruct((tokens, HD // 2), jnp.float32)
    return pl.pallas_call(
        functools.partial(gather_kernel, shards, heads, levels),
        out_shape=[
            jax.ShapeDtypeStruct((tokens, wide), low),
            jax.ShapeDtypeStruct((tokens, wide), low),
            jax.ShapeDtypeStruct((SLOTS, tokens, narrow), low),
            jax.ShapeDtypeStruct((SLOTS, tokens, narrow), low),
            jax.ShapeDtypeStruct((2 * (levels + 1),), jnp.int32),
            angle,
            angle,
        ],
        in_specs=[smem] + [hbm] * 4,
        out_specs=[vmem, vmem, hbm, hbm, smem, vmem, vmem],
        scratch_shapes=[
            pltpu.VMEM(q.shape, low),
            pltpu.VMEM(k.shape, low),
            pltpu.VMEM(v.shape, low),
            pltpu.VMEM(g.shape, low),
            pltpu.VMEM(q.shape, low),
            pltpu.VMEM(k.shape, low),
            pltpu.VMEM((SLOTS, tokens, narrow), low),
            pltpu.VMEM((SLOTS, tokens, narrow), low),
            pltpu.SemaphoreType.DMA((4,)),
            pltpu.SemaphoreType.DMA((2, SPLIT * heads, SLOTS)),
            pltpu.SemaphoreType.DMA((4, heads - 1)),
            pltpu.SemaphoreType.DMA((4, heads - 1)),
            pltpu.SemaphoreType.DMA((4,)),
            pltpu.SemaphoreType.DMA((28 * SPLIT * heads,)),
            pltpu.SemaphoreType.DMA((2, SPLIT * heads, SLOTS)),
        ],
        compiler_params=pltpu.CompilerParams(
            collective_id=0, has_side_effects=True, vmem_limit_bytes=VMEM_LIMIT
        ),
        name="gather",
    )(gap, q, k, v, g)


def attend_kernel(levels, table, *refs):
    q, g = refs[:2]
    keys, values = refs[2 : 3 + levels], refs[3 + levels : 4 + 2 * levels]
    cosine, sine, out, grad_q, part_k, part_v = refs[4 + 2 * levels :]
    tokens = q.shape[0]
    scaling = HD**-0.5
    f32, low = jnp.float32, jnp.bfloat16
    query = jnp.concatenate([q[:, i * HD : (i + 1) * HD] for i in range(GROUP)], 0)
    query = query * jnp.asarray(scaling, low)
    grad = jnp.concatenate([g[:, i * HD : (i + 1) * HD] for i in range(GROUP)], 0)
    across = (((1,), (1,)), ((), ()))
    down = (((0,), (0,)), ((), ()))
    key_at = lax.broadcasted_iota(jnp.int32, (tokens, tokens), 1)
    query_at = lax.broadcasted_iota(jnp.int32, (tokens, tokens), 0)
    later = jnp.concatenate([(key_at - query_at).astype(f32)] * GROUP, 0) > 0
    scores = []
    for j in range(levels + 1):
        s = lax.dot_general(query, keys[j][0], across, preferred_element_type=f32)
        if j == 0:
            s = jnp.where(later, -1e30, s)
        elif j == levels:
            s = jnp.where(later, s, -1e30)
        scores.append(s)
    absent = [jnp.where(table[levels + 1 + j] > 0, 0.0, 1e30) for j in range(levels + 1)]
    highest = functools.reduce(
        jnp.maximum, [jnp.max(s, -1, keepdims=True) - a for s, a in zip(scores, absent)]
    )
    raw = [jnp.exp(s - (highest + a)) for s, a in zip(scores, absent)]
    total = sum(jnp.sum(r, -1, keepdims=True) for r in raw)
    inverse = 1.0 / total
    probs = [r * inverse for r in raw]
    probs_low = [p.astype(low) for p in probs]
    attended = sum(
        lax.dot(p, values[j][0], preferred_element_type=f32) for j, p in enumerate(probs_low)
    )
    grad_probs = [
        lax.dot_general(grad, values[j][0], across, preferred_element_type=f32)
        for j in range(levels + 1)
    ]
    delta = sum(jnp.sum(p * d, -1, keepdims=True) for p, d in zip(probs, grad_probs))
    grad_scores = [
        (p * (d - delta)).astype(low) for p, d in zip(probs, grad_probs)
    ]
    turned = scaling * sum(
        lax.dot(d, keys[j][0], preferred_element_type=f32) for j, d in enumerate(grad_scores)
    )
    cos, sin = cosine[...], -sine[...]
    for i in range(GROUP):
        rows, at = slice(i * tokens, (i + 1) * tokens), slice(i * HD, (i + 1) * HD)
        out[:, at] = attended[rows].astype(low)
        grad_q[:, at] = turn(turned[rows], cos, sin).astype(low)
    part_k[...] = jnp.zeros_like(part_k)
    part_v[...] = jnp.zeros_like(part_v)
    for j in range(levels + 1):

        def put(j=j):
            slot = table[j]
            part_k[slot] = lax.dot_general(
                grad_scores[j], query, down, preferred_element_type=f32
            ).astype(low)
            part_v[slot] = lax.dot_general(
                probs_low[j], grad, down, preferred_element_type=f32
            ).astype(low)

        pl.when(table[levels + 1 + j] > 0)(put)


def attend(levels, table, qh, gh, kb, vb, cosine, sine):
    tokens = qh.shape[0]
    kv_local = kb.shape[2] // HD
    low = jnp.bfloat16

    def chosen(j):
        return pl.BlockSpec((1, tokens, HD), lambda h, t: (t[j], 0, h))

    wide = pl.BlockSpec((tokens, GROUP * HD), lambda h, t: (0, h))
    table_spec = pl.BlockSpec((tokens, HD // 2), lambda h, t: (0, 0))
    part = pl.BlockSpec((SLOTS, tokens, HD), lambda h, t: (0, 0, h))
    count = levels + 1
    return pl.pallas_call(
        functools.partial(attend_kernel, levels),
        out_shape=[
            jax.ShapeDtypeStruct(qh.shape, low),
            jax.ShapeDtypeStruct(qh.shape, low),
            jax.ShapeDtypeStruct(kb.shape, low),
            jax.ShapeDtypeStruct(vb.shape, low),
        ],
        grid_spec=pltpu.PrefetchScalarGridSpec(
            num_scalar_prefetch=1,
            grid=(kv_local,),
            in_specs=[wide, wide]
            + [chosen(j) for j in range(count)] * 2
            + [table_spec, table_spec],
            out_specs=[wide, wide, part, part],
        ),
        compiler_params=pltpu.CompilerParams(vmem_limit_bytes=VMEM_LIMIT),
        name="attend",
    )(table, qh, gh, *[kb] * count, *[vb] * count, cosine, sine)


def return_kernel(
    shards, heads, out, grad_q, part_k, part_v, cosine, sine, out_o, out_q, out_k, out_v,
    acc, odd, from_core, from_row, from_up, done, a_sem, b_sem, y_send, y_recv, y_local,
    p_send, p_recv, p_local, c_send, c_recv,
):
    parts = (part_k, part_v)
    loads, odd_loads = {}, {}
    for i in (3, 2, 1, 0):
        for kv in (0, 1):
            odd_loads[kv, i] = pltpu.make_async_copy(
                parts[kv].at[2 * i + 1], odd.at[kv, i], b_sem.at[kv, i]
            )
            odd_loads[kv, i].start()
    for at in (3, 4, 1, 2, 0):
        for kv in (0, 1):
            loads[kv, at] = pltpu.make_async_copy(
                parts[kv].at[2 * at], acc.at[kv, at], a_sem.at[kv, at]
            )
            loads[kv, at].start()
    me, head, core, row = greet(shards, heads)
    rows = out_o.shape[0]
    f32, low = jnp.float32, jnp.bfloat16
    exchanged = []

    def group(step):
        return pl.ds(pl.multiple_of(lax.rem(head + 1 + step, heads) * rows, rows), rows)

    def piece(step):
        size = rows // SPLIT
        start = lax.rem(head + 1 + step // SPLIT, heads) * rows + step % SPLIT * size
        return pl.ds(pl.multiple_of(start, size), size)

    def exchange(src, dst):
        index = len(exchanged)
        width = src.shape[1]
        columns = pl.ds(pl.multiple_of(head * width, width), width)
        copies = []
        for step in range(1, heads):
            peer = lax.rem(head + step, heads)
            copies.append(
                remote(
                    src.at[group(step - 1), :], dst.at[:, columns],
                    y_send.at[index, step - 1], y_recv.at[index, step - 1], {"head": peer},
                )
            )
        local = pltpu.make_async_copy(
            src.at[group(heads - 1), :], dst.at[:, columns], y_local.at[index]
        )
        for copy in copies:
            copy.start()
        local.start()
        exchanged.append((copies, local))

    chunks = [(kv, step) for step in range(SPLIT * heads) for kv in (0, 1)]
    core_copies, row_copies, down_copies = {}, {}, {}
    for pair in ((3, 2), (1, 0)):
        for kv, step in chunks:
            at = piece(step)
            for i in pair:
                if step == 0:
                    odd_loads[kv, i].wait()
                core_copies[kv, step, i] = remote(
                    odd.at[kv, i, at, :], from_core.at[kv, i, at, :],
                    c_send.at[kv, step, i], c_recv.at[kv, step, i],
                    {"ctx": me + 1 - 2 * core},
                )
                core_copies[kv, step, i].start()

    def to_row(chunk, i, slot):
        kv, step = chunk
        at = piece(step)
        row_copies[kv, step, i] = remote(
            acc.at[kv, slot // 2, at, :], from_row.at[kv, i, at, :],
            c_send.at[kv, step, 4 + i], c_recv.at[kv, step, 4 + i],
            {"ctx": me + 2 - 4 * row},
        )
        row_copies[kv, step, i].start()

    has_down, has_up = me >= 4, me + 4 < shards

    def to_down(chunk, i, slot):
        kv, step = chunk
        at = piece(step)
        down_copies[kv, step, i] = remote(
            acc.at[kv, slot // 2, at, :], from_up.at[kv, i, at, :],
            c_send.at[kv, step, 6 + i], c_recv.at[kv, step, 6 + i], {"ctx": me - 4},
        )
        pl.when(has_down)(down_copies[kv, step, i].start)

    def add(chunk, slot, pieces, i):
        kv, step = chunk
        at = piece(step)
        total = acc[kv, slot // 2, at, :].astype(f32) + pieces[kv, i, at, :].astype(f32)
        acc[kv, slot // 2, at, :] = total.astype(low)

    def add_when(condition, *args):
        pl.when(condition)(lambda: add(*args))

    for copy in loads.values():
        copy.wait()
    for chunk in chunks:
        core_copies[*chunk, 3].wait_recv()
        core_copies[*chunk, 2].wait_recv()
        add(chunk, 6, from_core, 3 - core)
        to_row(chunk, 1, 6)
        add_when(core == 1, chunk, 8, from_core, 3)
    exchange(out, out_o)
    exchange(grad_q, out_q)
    for chunk in chunks:
        core_copies[*chunk, 1].wait_recv()
        core_copies[*chunk, 0].wait_recv()
        add(chunk, 2, from_core, 1 - core)
        to_row(chunk, 0, 2)
        add(chunk, 4, from_core, 2 - core)
        add_when(core == 0, chunk, 0, from_core, 0)
    for chunk in chunks:
        row_copies[*chunk, 1].wait_recv()
        add_when(row == 1, chunk, 8, from_row, 1)
        to_down(chunk, 1, 8)
        add_when(row == 0, chunk, 4, from_row, 1)

    def middle(chunk):
        row_copies[*chunk, 0].wait_recv()
        add_when(row == 1, chunk, 4, from_row, 0)
        add_when(row == 0, chunk, 0, from_row, 0)

        @pl.when(has_up)
        def _():
            down_copies[*chunk, 1].wait_recv()
            add(chunk, 4, from_up, 1)

        to_down(chunk, 0, 4)

    finals = []

    def final(chunk):
        kv, step = chunk
        at = piece(step)

        @pl.when(has_up)
        def _():
            down_copies[*chunk, 0].wait_recv()
            add(chunk, 0, from_up, 0)

        if kv == 0:
            cos, sin = cosine[at, :], -sine[at, :]
            for i in range(acc.shape[3] // HD):
                col = slice(i * HD, (i + 1) * HD)
                done[kv, at, col] = turn(acc[kv, 0, at, col].astype(f32), cos, sin).astype(low)
        else:
            done[kv, at, :] = acc[kv, 0, at, :]
        width = acc.shape[3]
        size = rows // SPLIT
        part = slice(step % SPLIT * size, (step % SPLIT + 1) * size)
        dst = (out_k, out_v)[kv].at[part, pl.ds(pl.multiple_of(head * width, width), width)]
        if step // SPLIT == heads - 1:
            copy = pltpu.make_async_copy(done.at[kv, at, :], dst, p_local.at[kv, step % SPLIT])
        else:
            copy = remote(
                done.at[kv, at, :], dst, p_send.at[kv, step], p_recv.at[kv, step],
                {"head": lax.rem(head + 1 + step // SPLIT, heads)},
            )
        copy.start()
        finals.append(copy)

    for chunk, before in zip(chunks + [None], [None] + chunks):
        if chunk is not None:
            middle(chunk)
        if before is not None:
            final(before)
    for copies, local in exchanged:
        for copy in copies:
            copy.wait()
        local.wait()
    for copies in (core_copies, row_copies):
        for copy in copies.values():
            copy.wait_send()
    for copy in down_copies.values():
        pl.when(has_down)(copy.wait_send)
    for copy in finals:
        copy.wait()


def give_back(shards, heads, out, grad_q, part_k, part_v, cosine, sine):
    tokens, narrow = part_k.shape[1:]
    rows = tokens // heads
    low = jnp.bfloat16
    vmem = pl.BlockSpec(memory_space=pltpu.VMEM)
    hbm = pl.BlockSpec(memory_space=pltpu.HBM)
    wide_out = jax.ShapeDtypeStruct((rows, out.shape[1] * heads), low)
    narrow_out = jax.ShapeDtypeStruct((rows, narrow * heads), low)
    peers = heads - 1
    return pl.pallas_call(
        functools.partial(return_kernel, shards, heads),
        out_shape=[wide_out, wide_out, narrow_out, narrow_out],
        in_specs=[vmem, vmem, hbm, hbm, vmem, vmem],
        out_specs=[vmem] * 4,
        scratch_shapes=[
            pltpu.VMEM((2, 5, tokens, narrow), low),
            pltpu.VMEM((2, 4, tokens, narrow), low),
            pltpu.VMEM((2, 4, tokens, narrow), low),
            pltpu.VMEM((2, 2, tokens, narrow), low),
            pltpu.VMEM((2, 2, tokens, narrow), low),
            pltpu.VMEM((2, tokens, narrow), low),
            pltpu.SemaphoreType.DMA((2, 5)),
            pltpu.SemaphoreType.DMA((2, 4)),
            pltpu.SemaphoreType.DMA((2, peers)),
            pltpu.SemaphoreType.DMA((2, peers)),
            pltpu.SemaphoreType.DMA((2,)),
            pltpu.SemaphoreType.DMA((2, SPLIT * peers)),
            pltpu.SemaphoreType.DMA((2, SPLIT * peers)),
            pltpu.SemaphoreType.DMA((2, SPLIT)),
            pltpu.SemaphoreType.DMA((2, SPLIT * heads, 8)),
            pltpu.SemaphoreType.DMA((2, SPLIT * heads, 8)),
        ],
        compiler_params=pltpu.CompilerParams(
            collective_id=1, has_side_effects=True, vmem_limit_bytes=VMEM_LIMIT
        ),
        name="give_back",
    )(out, grad_q, part_k, part_v, cosine, sine)


def settle_kernel(count, *refs):
    given, made, held = refs[:count], refs[count : 2 * count], refs[2 * count : 3 * count]
    into, away = refs[3 * count :]
    loads = [pltpu.make_async_copy(given[i], held[i], into.at[i]) for i in range(count)]
    stores = [pltpu.make_async_copy(held[i], made[i], away.at[i]) for i in range(count)]
    for load in loads:
        load.start()
    for load, store in zip(loads, stores):
        load.wait()
        store.start()
    for store in stores:
        store.wait()


def settle(*arrays):
    count = len(arrays)
    space = pl.BlockSpec(memory_space=pltpu.HBM)
    return pl.pallas_call(
        functools.partial(settle_kernel, count),
        out_shape=[jax.ShapeDtypeStruct(a.shape, a.dtype) for a in arrays],
        in_specs=[space] * count,
        out_specs=[space] * count,
        scratch_shapes=[pltpu.VMEM(a.shape, a.dtype) for a in arrays]
        + [pltpu.SemaphoreType.DMA((count,))] * 2,
        compiler_params=pltpu.CompilerParams(vmem_limit_bytes=VMEM_LIMIT),
        name="settle",
    )(*arrays)


def run(shards, heads, queries, keys, values, grad_attn, parent_gap):
    tokens = queries.shape[0] * heads
    levels = WINDOW // tokens
    assert levels * FORK == SLOTS - 1 and shards % 4 == 0
    qh, gh, kb, vb, table, cosine, sine = gather(
        shards, heads, levels, parent_gap, queries, keys, values, grad_attn
    )
    out, grad_q, part_k, part_v = attend(levels, table, qh, gh, kb, vb, cosine, sine)
    return tuple(settle(*give_back(shards, heads, out, grad_q, part_k, part_v, cosine, sine)))


def solution(mesh):
    rows = P(("ctx", "head"), None)
    return jax.shard_map(
        functools.partial(run, mesh.shape["ctx"], mesh.shape["head"]),
        mesh=mesh,
        in_specs=(rows, rows, rows, rows, P()),
        out_specs=(rows, rows, rows, rows),
        check_vma=False,
    )
```
